512 devices in a mesh: grp: 64 (over y_hi, x, z), blk: 8 (over y_lo, core).
Axes of the slice: x: 4, y: 8 (y_hi: 2, y_lo: 4; y = y_hi * 4 + y_lo), z: 8, core: 2. Of those that a mesh axis runs over, the one named last changes fastest.
Arguments:
- features: float32 [65536, 256], P(('grp', 'blk')), may hold values from -1.5 to 1.5
- factor_u: float32 [65536, 128], P(('grp', 'blk')), may hold values from -1.8 to 1.8
- factor_v: float32 [65536, 128], P(('grp', 'blk')), may hold values from -1.8 to 1.8
- tile_mask: int32 [512, 512], P(('grp', 'blk')), may hold values 0 or 1
- matching: int32 [3, 64], replicated, may hold values from 0 to 63, each once within a row
Outputs:
- u_new: float32 [65536, 128], P(('grp', 'blk'))
- held_v: float32 [65536, 128], P(('grp', 'blk'))
The draws below stay inside these ranges and needn't reach their ends.
Inputs may be any that keep to these rules, and one draw needn't show every extreme that they name: `matching`: each row is a permutation of the 64 groups.
All inputs are finite; a program needn't handle non-finite values. No bound on the sum of `tile_mask` on one device may be relied on, other than what follows from the above.
Results may differ from the reference program's by a relative error of at most 0.017.
Values may be sent and summed in bfloat16 or wider, within the bound.
No kernel may reach another device: no remote copies, remote signals or barrier semaphores. Data moves between devices by JAX's collectives and lax.ppermute only.
A program may use at most 64 MiB of HBM per device.

```python
import jax
import jax.numpy as jnp
from jax import lax

F = 256
RANK = 128
TILE = 128
TPD = 1
SUB = 4
GROUPS = 64
NROWS = 65536
NTILES = 512
N_GRP = 64
N_BLK = 8


def draw_features(key, part):
    key = jax.random.fold_in(key, 11)
    return 0.25 * jax.random.truncated_normal(key, -6.0, 6.0, (NROWS, F), jnp.float32)


def draw_factor_u(key, part):
    key = jax.random.fold_in(key, 23)
    return 0.3 * jax.random.truncated_normal(key, -6.0, 6.0, (NROWS, RANK), jnp.float32)


def draw_factor_v(key, part):
    key = jax.random.fold_in(key, 37)
    return 0.3 * jax.random.truncated_normal(key, -6.0, 6.0, (NROWS, RANK), jnp.float32)


def set_ends(drawn, own_key, least, high):
    longest = drawn.shape.index(max(drawn.shape))
    spots = []
    for shift in (0, 1):
        where = [jax.random.randint(jax.random.fold_in(own_key, axis), (), 0, length) for axis, length in enumerate(drawn.shape)]
        where[longest] = (where[longest] + shift) % drawn.shape[longest]
        spots.append(tuple(where))
    return drawn.at[spots[0]].set(least).at[spots[1]].set(high)


def setup_inputs(seed: int = 0) -> dict:
    arg_keys = jax.random.split(jax.random.key(seed), 6)
    return {
        "features": draw_features(jax.random.fold_in(arg_keys[5], 71), 0),
        "factor_u": draw_factor_u(jax.random.fold_in(arg_keys[5], 71), 0),
        "factor_v": draw_factor_v(jax.random.fold_in(arg_keys[5], 71), 0),
        "tile_mask": set_ends((jax.random.randint(arg_keys[3], (NTILES, NTILES), 0, 2) < 1).astype(jnp.int32), jax.random.fold_in(arg_keys[3], 1), 0, 1),
        "matching": jax.vmap(lambda own: jax.random.permutation(own, GROUPS))(jax.random.split(arg_keys[4], (SUB - 1))).reshape((SUB - 1, GROUPS)).astype(jnp.int32),
    }


def pair_mats(left_rows, right_rows):
    return jnp.einsum("pnk,pmk->pnm", left_rows.astype(jnp.float32), right_rows.astype(jnp.float32), precision=lax.Precision.HIGHEST)


def invert(destinations, group_count):
    labels = jnp.arange(group_count, dtype=jnp.int32)
    matches = (destinations[None, :] == labels[:, None]).astype(jnp.int32)
    return jnp.sum(matches * labels[None, :], axis=1).astype(jnp.int32)


def reference(features, factor_u, factor_v, tile_mask, matching):
    groups = N_GRP
    blocks = N_BLK
    slot_rows = TPD * TILE
    slots = groups * blocks
    step_size = 4.0 / slot_rows
    xb = features.astype(jnp.bfloat16)
    left_factor = factor_u.reshape(slots, slot_rows, RANK)
    work_v = factor_v.reshape(groups, blocks, slot_rows, RANK)
    work_x = xb.reshape(groups, blocks, slot_rows, F)
    own_x = xb.reshape(slots, slot_rows, F)
    holdings = jnp.arange(groups, dtype=jnp.int32)
    tiles = tile_mask.reshape(slots, TPD, slots, TPD)
    slot_ids = jnp.arange(slots, dtype=jnp.int32)
    part_ids = slot_ids % blocks
    group_ids = slot_ids // blocks
    for sub_epoch in range(SUB):
        for cycle_step in range(blocks):
            columns = (holdings[group_ids] * blocks + (part_ids - cycle_step) % blocks).astype(jnp.int32)
            picked = tiles[slot_ids, :, columns, :].astype(jnp.float32)
            keeping = jnp.broadcast_to(picked[:, :, None, :, None], (slots, TPD, TILE, TPD, TILE)).reshape(slots, slot_rows, slot_rows)
            slot_v = work_v.reshape(slots, slot_rows, RANK)
            slot_x = work_x.reshape(slots, slot_rows, F)
            similar = pair_mats(own_x, slot_x)
            u_bf = left_factor.astype(jnp.bfloat16)
            v_bf = slot_v.astype(jnp.bfloat16)
            predicted = pair_mats(u_bf, v_bf)
            residual = (keeping * (predicted - similar)).astype(jnp.bfloat16)
            grad_u = jnp.einsum("pnm,pmk->pnk", residual.astype(jnp.float32), v_bf.astype(jnp.float32), precision=lax.Precision.HIGHEST)
            grad_v = jnp.einsum("pnm,pnk->pmk", residual.astype(jnp.float32), u_bf.astype(jnp.float32), precision=lax.Precision.HIGHEST)
            left_factor = left_factor - step_size * grad_u
            slot_v = slot_v - step_size * grad_v
            work_v = jnp.roll(slot_v.reshape(groups, blocks, slot_rows, RANK), 1, axis=1)
            work_x = jnp.roll(work_x, 1, axis=1)
        if sub_epoch + 1 < SUB:
            inverse = invert(matching[sub_epoch], groups)
            work_v = work_v[inverse]
            work_x = work_x[inverse]
            holdings = holdings[inverse]
    return left_factor.reshape(NROWS, RANK), work_v.reshape(NROWS, RANK)
```

```python
import functools

import jax
import jax.numpy as jnp
from jax import lax
from jax.experimental import pallas as pl
from jax.experimental.pallas import tpu as pltpu
from jax.sharding import Mesh, PartitionSpec as P

SUB = 4
GRP = ("yh", "x", "z")
BLK = ("yl", "core")
ALL = GRP + BLK
BF = jnp.bfloat16
F32 = jnp.float32
LANES = 128
SMEM = pl.BlockSpec(memory_space=pltpu.SMEM)
VMEM = pl.BlockSpec(memory_space=pltpu.VMEM)


def tables_kernel(groups, leaves, levels, matching_ref, leaf_ref, node_ref, held_ref, inv_ref):
    def invert(e, carry):
        for t in range(levels - 1):
            inv_ref[t * groups + matching_ref[t, e]] = e
        return carry

    lax.fori_loop(0, groups, invert, 0)

    def trace_back(d, carry):
        held = [d]
        for t in range(1, levels):
            e = d
            for s in range(t - 1, -1, -1):
                e = inv_ref[s * groups + e]
            held.append(e)
        for t in range(levels):
            held_ref[t * groups + d] = held[t]
        nodes = {(): d}
        for t in range(levels - 2, -1, -1):
            for path in [p for p in nodes if len(p) == levels - 2 - t]:
                nodes[path + (0,)] = nodes[path]
                nodes[path + (1,)] = inv_ref[t * groups + nodes[path]]
        for k in range(leaves):
            bits = tuple((k >> (levels - 2 - i)) & 1 for i in range(levels - 1))
            leaf_ref[d * leaves + k] = nodes[bits]
            for t in range(levels):
                node_ref[(d * leaves + k) * levels + t] = nodes[bits[: levels - 1 - t]]
        return carry

    lax.fori_loop(0, groups, trace_back, 0)


def tables_call(matching, leaves):
    levels, groups = matching.shape[0] + 1, matching.shape[1]
    return pl.pallas_call(
        functools.partial(tables_kernel, groups, leaves, levels),
        out_shape=(
            jax.ShapeDtypeStruct((groups * leaves,), jnp.int32),
            jax.ShapeDtypeStruct((groups * leaves * levels,), jnp.int32),
            jax.ShapeDtypeStruct((groups * levels,), jnp.int32),
        ),
        in_specs=[SMEM],
        out_specs=(SMEM, SMEM, SMEM),
        scratch_shapes=[pltpu.SMEM((groups * (levels - 1),), jnp.int32)],
        cost_estimate=pl.CostEstimate(flops=2000000, bytes_accessed=4096, transcendentals=0),
    )(matching)


def pick_kernel(leaves, leaf_ref, pieces_ref, out_ref):
    def one(d, carry):
        for k in range(leaves):
            out_ref[d, k] = pieces_ref[leaf_ref[d * leaves + k]]
        return carry

    lax.fori_loop(0, out_ref.shape[0], one, 0)


def pick_call(leaf_table, pieces, leaves):
    groups = pieces.shape[0]
    return pl.pallas_call(
        functools.partial(pick_kernel, leaves),
        out_shape=jax.ShapeDtypeStruct((groups, leaves) + pieces.shape[1:], pieces.dtype),
        in_specs=[SMEM, VMEM],
        out_specs=VMEM,
        compiler_params=pltpu.CompilerParams(vmem_limit_bytes=16 << 20),
        cost_estimate=pl.CostEstimate(flops=1000000, bytes_accessed=2 << 20, transcendentals=0),
    )(leaf_table, pieces)


def sub_epoch_kernel(blocks, step_size, level, last, info_ref, keep_ref, *refs):
    if level == 0:
        x_ref, uv_ref, *refs = refs
    else:
        left_ref, right_ref, xl_ref, xr_ref, *refs = refs
    *outs, ls, rs, lb, rb = refs
    rank = ls.shape[2]
    for b in range(blocks):
        if level == 0:
            left, right = uv_ref[b, 0], uv_ref[b, 1]
            ls[b], rs[b] = left.astype(F32), right.astype(F32)
            lx = rx = x_ref
        else:
            left, right = left_ref[b].astype(BF), right_ref[b]
            ls[b], rs[b] = left_ref[b], right.astype(F32)
            lx, rx = xl_ref, xr_ref
        lb[b, :, :rank], rb[b, :, :rank] = left, right
        for half in range(2):
            span = slice((half + 1) * rank, (half + 2) * rank)
            lb[b, :, span] = lx[b, half]
            rb[b, :, span] = -rx[b, half]
    flip = info_ref[1 + level]

    def cycle_step(step, carry):
        shift = jnp.where(flip == 1, step, blocks - step)
        places = [lax.rem(b + shift, blocks) for b in range(blocks)]
        diffs = [
            lax.dot_general(lb[b], rb[places[b]], (((1,), (1,)), ((), ())), preferred_element_type=F32)
            for b in range(blocks)
        ]
        resids = []
        for b in range(blocks):
            row = jnp.where(flip == 1, places[b], b)
            col = jnp.where(flip == 1, b, places[b])
            resids.append((keep_ref[row, level * blocks + col] * diffs[b]).astype(BF))
        grads_l = [
            jnp.dot(resids[b], rb[places[b], :, :rank], preferred_element_type=F32) for b in range(blocks)
        ]
        grads_r = [
            lax.dot_general(resids[b], lb[b, :, :rank], (((0,), (0,)), ((), ())), preferred_element_type=F32)
            for b in range(blocks)
        ]
        for b in range(blocks):
            new_left = ls[b] - step_size * grads_l[b]
            ls[b] = new_left
            lb[b, :, :rank] = new_left.astype(BF)
        for b in range(blocks):
            new_right = rs[places[b]] - step_size * grads_r[b]
            rs[places[b]] = new_right
            rb[places[b], :, :rank] = new_right.astype(BF)
        return carry

    lax.fori_loop(0, blocks, cycle_step, 0)
    me = info_ref[0]
    if last:
        uo_ref, vo_ref = outs

        @pl.when(flip == 0)
        def _():
            uo_ref[...] = ls[me]
            vo_ref[...] = rs[me]

        @pl.when(flip == 1)
        def _():
            uo_ref[...] = rs[me]
            vo_ref[...] = ls[me]
    else:
        kept_ref, sent_ref = outs
        same = info_ref[2 + level] == flip

        @pl.when(same)
        def _():
            kept_ref[...] = ls[...]
            sent_ref[...] = lb[:, :, :rank]

        @pl.when(jnp.logical_not(same))
        def _():
            kept_ref[...] = rs[...]
            sent_ref[...] = rb[:, :, :rank]


def sub_epoch_call(level, last, info, keeps, *arrays):
    blocks, _, slot_rows, rank = arrays[-1].shape
    whole = (blocks, slot_rows, rank)
    if last:
        outs = (jax.ShapeDtypeStruct((slot_rows, rank), F32),) * 2
    else:
        outs = (jax.ShapeDtypeStruct(whole, F32), jax.ShapeDtypeStruct(whole, BF))
    state, operand = pltpu.VMEM(whole, F32), pltpu.VMEM((blocks, slot_rows, 3 * rank), BF)
    return pl.pallas_call(
        functools.partial(sub_epoch_kernel, blocks, 4.0 / slot_rows, level, last),
        out_shape=outs,
        in_specs=[SMEM, SMEM] + [VMEM] * len(arrays),
        out_specs=(VMEM, VMEM),
        scratch_shapes=[state, state, operand, operand],
        compiler_params=pltpu.CompilerParams(vmem_limit_bytes=24 << 20),
        cost_estimate=pl.CostEstimate(
            flops=2 * blocks * blocks * slot_rows * slot_rows * 5 * rank,
            bytes_accessed=4 << 20,
            transcendentals=0,
        ),
    )(info, keeps, *arrays)


def swapped(array, bit, count):
    return lax.ppermute(array, BLK, [(i, i ^ (1 << bit)) for i in range(count)])


def local(features, factor_u, factor_v, tile_mask, matching):
    groups = lax.axis_size(GRP)
    blocks = lax.axis_size(BLK)
    group = lax.axis_index(GRP)
    part = lax.axis_index(BLK).astype(jnp.int32)
    slot_rows, rank = factor_u.shape
    piece_rows = 4 * slot_rows // groups

    packed = jnp.concatenate([features[:, :rank], features[:, rank:], factor_u, factor_v], axis=0).astype(BF)
    pieces = packed.reshape(groups, piece_rows, rank)
    pieces = lax.all_to_all(pieces, GRP, split_axis=0, concat_axis=0, tiled=True)

    leaf_table, node_table, held_table = tables_call(matching, blocks)
    held = lax.dynamic_index_in_dim(held_table.reshape(SUB, groups), group, 1, keepdims=False)
    row = jnp.take(tile_mask.reshape(groups, blocks).astype(F32), held, axis=0).reshape(1, 1, SUB * blocks)
    row = jnp.broadcast_to(jnp.pad(row, ((0, 0), (0, 0), (0, LANES - SUB * blocks))), (groups, 1, LANES))
    rows = lax.all_to_all(row, GRP, split_axis=0, concat_axis=0, tiled=True)[:, 0, : SUB * blocks]
    nodes = lax.dynamic_index_in_dim(node_table.reshape(groups, blocks * SUB), group, 0, keepdims=False)
    picked = jnp.take(rows, nodes, axis=0).reshape(blocks, SUB, SUB, blocks)
    picked = jnp.stack([picked[:, t, t] for t in range(SUB)], axis=1).reshape(blocks, 1, SUB * blocks)
    picked = jnp.pad(picked, ((0, 0), (0, 0), (0, LANES - SUB * blocks)))
    keeps = lax.all_to_all(picked, BLK, split_axis=0, concat_axis=0, tiled=True)[:, 0, : SUB * blocks]

    sends = pick_call(leaf_table, pieces, blocks)
    got = lax.all_to_all(sends, GRP, split_axis=0, concat_axis=0, tiled=True)
    got = jnp.transpose(got, (1, 0, 2, 3))
    half = groups // 2
    x = lax.all_to_all(got[:, :half], BLK, split_axis=0, concat_axis=0, tiled=True)
    uv = lax.all_to_all(got[:, half:], BLK, split_axis=0, concat_axis=0, tiled=True)
    x = x.reshape(blocks, 2, slot_rows, rank)
    uv = uv.reshape(blocks, 2, slot_rows, rank)

    bits = [(part >> t) & 1 for t in range(SUB - 1)]
    info = jnp.stack([part, jnp.zeros((), jnp.int32)] + bits)
    kept, sent = sub_epoch_call(0, False, info, keeps, x, uv)
    left_x = x
    for level in range(1, SUB):
        right_x = swapped(left_x, level - 1, blocks)
        right = swapped(sent, level - 1, blocks)
        last = level + 1 == SUB
        kept, sent = sub_epoch_call(level, last, info, keeps, kept, right, left_x, right_x)
        if not last:
            left_x = jnp.where(bits[level] == bits[level - 1], left_x, right_x)
    return kept, sent


def solution(mesh):
    fine = Mesh(mesh.devices.reshape(2, 4, 8, 4, 2), ALL)
    in_specs = (P(ALL, None), P(ALL, None), P(ALL, None), P(ALL, None), P())
    out_specs = (P(ALL, None), P(ALL, None))
    return jax.shard_map(local, mesh=fine, in_specs=in_specs, out_specs=out_specs, check_vma=False)
```

```python
import functools

import jax
import jax.numpy as jnp
from jax import lax
from jax.experimental import pallas as pl
from jax.experimental.pallas import tpu as pltpu
from jax.sharding import Mesh, PartitionSpec as P

SUB = 4
GRP = ("yh", "x", "z")
BLK = ("yl", "core")
ALL = GRP + BLK
FAR = ("yh", "yl", "z")
NEAR = ("x", "core")
YH, XS, ZS, YL, CORES = 2, 4, 8, 4, 2
GROUPS, PARTS = YH * XS * ZS, YL * CORES
BF = jnp.bfloat16
F32 = jnp.float32
LANES = 128
PIECE = 8
SMEM = pl.BlockSpec(memory_space=pltpu.SMEM)
VMEM = pl.BlockSpec(memory_space=pltpu.VMEM)


def pack_kernel(x_ref, u_ref, v_ref, out_ref):
    rows, rank = u_ref.shape
    out_ref[:rows] = x_ref[:, :rank].astype(BF)
    out_ref[rows : 2 * rows] = x_ref[:, rank:].astype(BF)
    out_ref[2 * rows : 3 * rows] = u_ref[...].astype(BF)
    out_ref[3 * rows :] = v_ref[...].astype(BF)


def pack_call(features, factor_u, factor_v):
    rows, rank = factor_u.shape
    return pl.pallas_call(
        pack_kernel,
        out_shape=jax.ShapeDtypeStruct((4 * rows, rank), BF),
        in_specs=[VMEM] * 3,
        out_specs=VMEM,
        cost_estimate=pl.CostEstimate(flops=100000, bytes_accessed=400000, transcendentals=0),
    )(features, factor_u, factor_v)


def mask_place(group, part):
    z = group % ZS
    return (group // (XS * ZS) * YL + part // CORES) * 2 + z // 4, (z % 4) * SUB * PARTS


def tables_kernel(here_ref, matching_ref, mask_ref, leaf_ref, info_ref, tile_ref, inv_ref):
    group, part = here_ref[0], here_ref[1]

    def invert(e, carry):
        for t in range(SUB - 1):
            inv_ref[t * GROUPS + matching_ref[t, e]] = e
        return carry

    lax.fori_loop(0, GROUPS, invert, 0, unroll=4)

    def before(t, e):
        return inv_ref[t * GROUPS + e]

    def trace_back(d, carry):
        nodes = [d]
        for t in range(SUB - 2, -1, -1):
            nodes = [n for e in nodes for n in (e, before(t, e))]
        base = (d // (XS * ZS) * YL * ZS + d % ZS) * PARTS + d // ZS % XS * CORES
        for k in range(PARTS):
            leaf_ref[base + k // CORES * ZS * PARTS + k % CORES] = nodes[k]
        return carry

    lax.fori_loop(0, GROUPS, trace_back, 0, unroll=2)

    info_ref[0] = part
    node = group
    for t in range(SUB - 1, -1, -1):
        info_ref[SUB + t] = node
        if t > 0:
            bit = part // (1 << (t - 1)) % 2
            info_ref[t] = bit
            node = jnp.where(bit == 1, before(t - 1, node), node)

    row, lane = mask_place(group, part)
    lanes = lax.broadcasted_iota(jnp.int32, (PIECE, LANES), 1)
    values = jnp.zeros((PIECE, LANES), jnp.int32)
    for t in range(SUB):
        held = group
        for s in range(t - 1, -1, -1):
            held = before(s, held)
        for c in range(PARTS):
            values = jnp.where(lanes == lane + t * PARTS + c, mask_ref[0, held * PARTS + c], values)
    rows = lax.broadcasted_iota(jnp.int32, (PIECE, LANES), 0)
    tile_ref[...] = jnp.where(rows == row % PIECE, values, 0).astype(F32).astype(BF)


def tables_call(here, matching, mask):
    return pl.pallas_call(
        tables_kernel,
        out_shape=(
            jax.ShapeDtypeStruct((GROUPS * PARTS,), jnp.int32),
            jax.ShapeDtypeStruct((2 * SUB,), jnp.int32),
            jax.ShapeDtypeStruct((PIECE, LANES), BF),
        ),
        in_specs=[SMEM, SMEM, SMEM],
        out_specs=(SMEM, SMEM, VMEM),
        scratch_shapes=[pltpu.SMEM((GROUPS * (SUB - 1),), jnp.int32)],
        cost_estimate=pl.CostEstimate(flops=2000000, bytes_accessed=4096, transcendentals=0),
    )(here, matching, mask)


def pick_kernel(leaf_ref, tile_ref, pieces_ref, out_ref):
    tile = tile_ref[...]

    def one(far, carry):
        for near in range(XS * CORES):
            out_ref[far, near] = pieces_ref[leaf_ref[far * XS * CORES + near]]
        out_ref[far, XS * CORES] = tile
        return carry

    lax.fori_loop(0, out_ref.shape[0], one, 0, unroll=4)


def pick_call(leaf_table, tile, pieces):
    return pl.pallas_call(
        pick_kernel,
        out_shape=jax.ShapeDtypeStruct((YH * YL * ZS, XS * CORES + 1, PIECE, LANES), BF),
        in_specs=[SMEM, VMEM, VMEM],
        out_specs=VMEM,
        compiler_params=pltpu.CompilerParams(vmem_limit_bytes=16 << 20),
        cost_estimate=pl.CostEstimate(flops=1000000, bytes_accessed=2 << 20, transcendentals=0),
    )(leaf_table, tile, pieces)


def regroup_kernel(got_ref, out_ref):
    far = YH * YL * ZS
    for near in range(XS * CORES):
        out_ref[near, :far] = got_ref[:, near]
    for yh in range(YH):
        span = far // YH
        total = jnp.sum(got_ref[yh * span : (yh + 1) * span, XS * CORES].astype(F32), axis=0).astype(BF)
        for near in range(XS * CORES):
            out_ref[near, far + yh] = total


def regroup_call(got):
    return pl.pallas_call(
        regroup_kernel,
        out_shape=jax.ShapeDtypeStruct((XS * CORES, YH * YL * ZS + YH, PIECE, LANES), BF),
        in_specs=[VMEM],
        out_specs=VMEM,
        compiler_params=pltpu.CompilerParams(vmem_limit_bytes=16 << 20),
        cost_estimate=pl.CostEstimate(flops=1000000, bytes_accessed=2 << 20, transcendentals=0),
    )(got)


def sim_kernel(xl_ref, xr_ref, out_ref, lx, rx):
    blocks, _, rows, _ = out_ref.shape
    rank, span = LANES, rows // 2
    for b in range(blocks):
        yl, core = b // CORES, b % CORES
        taken = pl.ds(yl * span, span)
        for i in range(2):
            put = pl.ds(b * rows + i * span, span)
            for half in range(2):
                near = (2 * half + i) * CORES + core
                lanes = slice(half * rank, (half + 1) * rank)
                lx[put, lanes] = xl_ref[near, taken]
                rx[put, lanes] = xr_ref[near, taken]
    for r in range(0, blocks, 2):
        right = rx[r * rows : (r + 2) * rows]
        for b in range(0, blocks, 2):
            sims = lax.dot_general(
                lx[b * rows : (b + 2) * rows], right, (((1,), (1,)), ((), ())), preferred_element_type=F32
            )
            for i in range(2):
                for j in range(2):
                    out_ref[b + i, r + j] = sims[i * rows : (i + 1) * rows, j * rows : (j + 1) * rows]


def sim_call(rows, left_x, right_x):
    operand = pltpu.VMEM((PARTS * rows, 2 * LANES), BF)
    return pl.pallas_call(
        sim_kernel,
        out_shape=jax.ShapeDtypeStruct((PARTS, PARTS, rows, rows), F32),
        in_specs=[VMEM, VMEM],
        out_specs=VMEM,
        scratch_shapes=[operand, operand],
        compiler_params=pltpu.CompilerParams(vmem_limit_bytes=24 << 20),
        cost_estimate=pl.CostEstimate(
            flops=4 * PARTS * PARTS * rows * rows * LANES, bytes_accessed=4 << 20, transcendentals=0
        ),
    )(left_x, right_x)


def sub_epoch_kernel(step_size, level, last, info_ref, mask_ref, sim_ref, *refs):
    if level == 0:
        all_ref, *refs = refs
    else:
        left_ref, right_ref, *refs = refs
    *outs, ls, rs, lb, rb, mf, kr, ks = refs
    blocks, rows, rank = ls.shape
    part, flip, node = info_ref[0], jnp.int32(0) if level == 0 else info_ref[level], info_ref[SUB + level]

    mf[...] = mask_ref[...].astype(F32)
    for b in range(blocks):
        row, lane = mask_place(node, b)
        kr[pl.ds(b, 1)] = mf[node // ZS % XS * CORES + b % CORES, pl.ds(row, 1)]
    values = kr[...]
    lanes = lax.broadcasted_iota(jnp.int32, values.shape, 1)
    for c in range(blocks):
        mine = jnp.where(lanes == lane + level * PARTS + c, values, 0.0)
        ks[c] = jnp.broadcast_to(jnp.sum(mine, axis=1, keepdims=True), values.shape)

    span = rows // 2
    for b in range(blocks):
        if level == 0:
            yl, core = b // CORES, b % CORES
            moved = pl.ds((YL + yl) * span, span)
            for i in range(2):
                put = pl.ds(i * span, span)
                left = all_ref[i * CORES + core, moved]
                right = all_ref[(2 + i) * CORES + core, moved]
                ls[b, put], rs[b, put] = left.astype(F32), right.astype(F32)
                lb[b, put], rb[b, put] = left, right
        else:
            ls[b], rs[b] = left_ref[b], right_ref[b].astype(F32)
            lb[b], rb[b] = left_ref[b].astype(BF), right_ref[b]

    def cycle_step(step, carry):
        shift = jnp.where(flip == 1, step, blocks - step)
        places = [lax.rem(b + shift, blocks) for b in range(blocks)]
        preds = [
            lax.dot_general(lb[b], rb[places[b]], (((1,), (1,)), ((), ())), preferred_element_type=F32)
            for b in range(blocks)
        ]
        resids = []
        for b in range(blocks):
            row = jnp.where(flip == 1, places[b], b)
            col = jnp.where(flip == 1, b, places[b])
            resids.append((ks[col, pl.ds(row, 1)] * (preds[b] - sim_ref[b, places[b]])).astype(BF))
        grads_l = [jnp.dot(resids[b], rb[places[b]], preferred_element_type=F32) for b in range(blocks)]
        grads_r = [
            lax.dot_general(resids[b], lb[b], (((0,), (0,)), ((), ())), preferred_element_type=F32)
            for b in range(blocks)
        ]
        for b in range(blocks):
            new_left = ls[b] - step_size * grads_l[b]
            ls[b] = new_left
            lb[b] = new_left.astype(BF)
        for b in range(blocks):
            new_right = rs[places[b]] - step_size * grads_r[b]
            rs[places[b]] = new_right
            rb[places[b]] = new_right.astype(BF)
        return carry

    lax.fori_loop(0, blocks, cycle_step, 0)
    if last:
        uo_ref, vo_ref = outs

        @pl.when(flip == 0)
        def _():
            uo_ref[...] = ls[part]
            vo_ref[...] = rs[part]

        @pl.when(flip == 1)
        def _():
            uo_ref[...] = rs[part]
            vo_ref[...] = ls[part]
    else:
        kept_ref, sent_ref = outs
        same = info_ref[1 + level] == flip

        @pl.when(same)
        def _():
            kept_ref[...] = ls[...]
            sent_ref[...] = lb[...]

        @pl.when(jnp.logical_not(same))
        def _():
            kept_ref[...] = rs[...]
            sent_ref[...] = rb[...]


def sub_epoch_call(level, rows, info, mask, sims, *arrays):
    rank, last = LANES, level + 1 == SUB
    whole = (PARTS, rows, rank)
    if last:
        outs = (jax.ShapeDtypeStruct((rows, rank), F32),) * 2
    else:
        outs = (jax.ShapeDtypeStruct(whole, F32), jax.ShapeDtypeStruct(whole, BF))
    return pl.pallas_call(
        functools.partial(sub_epoch_kernel, 4.0 / rows, level, last),
        out_shape=outs,
        in_specs=[SMEM] + [VMEM] * (2 + len(arrays)),
        out_specs=(VMEM, VMEM),
        scratch_shapes=[
            pltpu.VMEM(whole, F32),
            pltpu.VMEM(whole, F32),
            pltpu.VMEM(whole, BF),
            pltpu.VMEM(whole, BF),
            pltpu.VMEM(mask.shape, F32),
            pltpu.VMEM((PARTS, LANES), F32),
            pltpu.VMEM((PARTS, PARTS, LANES), F32),
        ],
        compiler_params=pltpu.CompilerParams(vmem_limit_bytes=28 << 20),
        cost_estimate=pl.CostEstimate(
            flops=2 * PARTS * PARTS * rows * rows * 3 * rank,
            bytes_accessed=6 << 20,
            transcendentals=0,
        ),
    )(info, mask, sims, *arrays)


def swapped(array, bit):
    return lax.ppermute(array, BLK, [(i, i ^ (1 << bit)) for i in range(PARTS)])


def spread(array, axes):
    return lax.all_to_all(array, axes, split_axis=0, concat_axis=0, tiled=True)


def halves_out(array, bit, core):
    half = array.shape[0] // 2
    return swapped(lax.dynamic_slice_in_dim(array, core * half, half, 0), bit)


def halves_in(first, core):
    second = swapped(first, 0)
    return jnp.where(core == 0, jnp.concatenate([first, second]), jnp.concatenate([second, first]))


def local(features, factor_u, factor_v, tile_mask, matching):
    group = lax.axis_index(GRP).astype(jnp.int32)
    part = lax.axis_index(BLK).astype(jnp.int32)
    slot_rows, rank = factor_u.shape
    bits = [(part >> t) & 1 for t in range(SUB - 1)]

    pieces = spread(pack_call(features, factor_u, factor_v).reshape(GROUPS, PIECE, rank), GRP)
    leaf_table, info, tile = tables_call(jnp.stack([group, part]), matching, tile_mask)
    got = spread(pick_call(leaf_table, tile, pieces), FAR)
    got = spread(regroup_call(got), NEAR).reshape(XS * CORES, -1, rank)
    half = YL * slot_rows // 2
    left_x = got[:, :half]
    mask = got[:, 2 * half :]

    coming_x = swapped(left_x, 0)
    kept, sent = sub_epoch_call(0, slot_rows, info, mask, sim_call(slot_rows, got, got), got)
    for level in range(1, SUB):
        right = swapped(sent, level - 1)
        kept, coming_x = lax.optimization_barrier((kept, coming_x))
        right_x = coming_x if level == 1 else halves_in(coming_x, bits[0])
        sims = sim_call(slot_rows, left_x, right_x)
        if level + 1 < SUB:
            left_x = jnp.where(bits[level] == bits[level - 1], left_x, right_x)
            coming_x = halves_out(left_x, level, bits[0])
        kept, sent = sub_epoch_call(level, slot_rows, info, mask, sims, kept, right)
    return kept, sent


def solution(mesh):
    fine = Mesh(mesh.devices.reshape(YH, XS, ZS, YL, CORES), ALL)
    in_specs = (P(ALL, None), P(ALL, None), P(ALL, None), P(ALL, None), P())
    out_specs = (P(ALL, None), P(ALL, None))
    return jax.shard_map(local, mesh=fine, in_specs=in_specs, out_specs=out_specs, check_vma=False)
```

```python
import functools

import jax
import jax.numpy as jnp
from jax import lax
from jax.experimental import pallas as pl
from jax.experimental.pallas import tpu as pltpu
from jax.sharding import Mesh, PartitionSpec as P

SUB = 4
GRP = ("yh", "x", "z")
BLK = ("yl", "core")
ALL = GRP + BLK
FAR = ("yh", "yl", "z")
NEAR = ("x", "core")
YH, XS, ZS, YL, CORES = 2, 4, 8, 4, 2
GROUPS, PARTS = YH * XS * ZS, YL * CORES
BF = jnp.bfloat16
F32 = jnp.float32
LANES = 128
PIECE = 8
STRIDES = (1, 2 * CORES, CORES)
INFO = GROUPS * PARTS
VALUES = INFO + 16
SMEM = pl.BlockSpec(memory_space=pltpu.SMEM)
VMEM = pl.BlockSpec(memory_space=pltpu.VMEM)


def pack_kernel(x_ref, u_ref, v_ref, out_ref):
    rows, rank = u_ref.shape
    out_ref[:rows] = x_ref[:, :rank].astype(BF)
    out_ref[rows : 2 * rows] = x_ref[:, rank:].astype(BF)
    out_ref[2 * rows : 3 * rows] = u_ref[...].astype(BF)
    out_ref[3 * rows :] = v_ref[...].astype(BF)


def pack_call(features, factor_u, factor_v):
    rows, rank = factor_u.shape
    return pl.pallas_call(
        pack_kernel,
        out_shape=jax.ShapeDtypeStruct((4 * rows, rank), BF),
        in_specs=[VMEM] * 3,
        out_specs=VMEM,
        cost_estimate=pl.CostEstimate(flops=100000, bytes_accessed=400000, transcendentals=0),
    )(features, factor_u, factor_v)


def mask_place(group, part):
    z = group % ZS
    return (group // (XS * ZS) * YL + part // CORES) * 2 + z // 4, (z % 4) * SUB * PARTS


def tables_kernel(here_ref, matching_ref, mask_ref, table_ref, inv_ref):
    group, part = here_ref[0], here_ref[1]

    def invert(e, carry):
        for t in range(SUB - 1):
            inv_ref[t * GROUPS + matching_ref[t, e]] = e
        return carry

    lax.fori_loop(0, GROUPS, invert, 0, unroll=4)

    def before(t, e):
        return inv_ref[t * GROUPS + e]

    def trace_back(d, carry):
        nodes = [d]
        for t in range(SUB - 2, -1, -1):
            nodes = [n for e in nodes for n in (e, before(t, e))]
        base = (d // (XS * ZS) * YL * ZS + d % ZS) * PARTS + d // ZS % XS * CORES
        for k in range(PARTS):
            yl, core = k // 2 % 2 * 2 + k // 4, k % 2
            table_ref[base + yl * ZS * PARTS + core] = nodes[k]
        return carry

    lax.fori_loop(0, GROUPS, trace_back, 0, unroll=2)

    table_ref[INFO] = part
    node = group
    for t in range(SUB - 1, -1, -1):
        table_ref[INFO + SUB + t] = node
        if t > 0:
            bit = part // STRIDES[t - 1] % 2
            table_ref[INFO + t] = bit
            node = jnp.where(bit == 1, before(t - 1, node), node)
    table_ref[INFO + 2 * SUB] = group
    for t in range(SUB):
        held = group
        for s in range(t - 1, -1, -1):
            held = before(s, held)
        for c in range(PARTS):
            table_ref[VALUES + t * PARTS + c] = mask_ref[0, held * PARTS + c]


def tables_call(here, matching, mask):
    return pl.pallas_call(
        tables_kernel,
        out_shape=jax.ShapeDtypeStruct((VALUES + SUB * PARTS,), jnp.int32),
        in_specs=[SMEM, SMEM, SMEM],
        out_specs=SMEM,
        scratch_shapes=[pltpu.SMEM((GROUPS * (SUB - 1),), jnp.int32)],
        cost_estimate=pl.CostEstimate(flops=2000000, bytes_accessed=4096, transcendentals=0),
    )(here, matching, mask)


def pick_kernel(table_ref, pieces_ref, out_ref):
    row, lane = mask_place(table_ref[INFO + 2 * SUB], table_ref[INFO])
    lanes = lax.broadcasted_iota(jnp.int32, (PIECE, LANES), 1)
    values = jnp.zeros((PIECE, LANES), jnp.int32)
    for i in range(SUB * PARTS):
        values = jnp.where(lanes == lane + i, table_ref[VALUES + i], values)
    rows = lax.broadcasted_iota(jnp.int32, (PIECE, LANES), 0)
    tile = jnp.where(rows == row % PIECE, values, 0).astype(F32).astype(BF)

    def one(far, carry):
        for near in range(XS * CORES):
            out_ref[far, near] = pieces_ref[table_ref[far * XS * CORES + near]]
        out_ref[far, XS * CORES] = tile
        return carry

    lax.fori_loop(0, out_ref.shape[0], one, 0, unroll=4)


def pick_call(table, pieces):
    return pl.pallas_call(
        pick_kernel,
        out_shape=jax.ShapeDtypeStruct((YH * YL * ZS, XS * CORES + 1, PIECE, LANES), BF),
        in_specs=[SMEM, VMEM],
        out_specs=VMEM,
        compiler_params=pltpu.CompilerParams(vmem_limit_bytes=16 << 20),
        cost_estimate=pl.CostEstimate(flops=1000000, bytes_accessed=2 << 20, transcendentals=0),
    )(table, pieces)


def regroup_kernel(got_ref, out_ref):
    far = YH * YL * ZS
    for near in range(XS * CORES):
        out_ref[near, :far] = got_ref[:, near]
    for yh in range(YH):
        span = far // YH
        total = jnp.sum(got_ref[yh * span : (yh + 1) * span, XS * CORES].astype(F32), axis=0).astype(BF)
        for near in range(XS * CORES):
            out_ref[near, far + yh] = total


def regroup_call(got):
    return pl.pallas_call(
        regroup_kernel,
        out_shape=jax.ShapeDtypeStruct((XS * CORES, YH * YL * ZS + YH, PIECE, LANES), BF),
        in_specs=[VMEM],
        out_specs=VMEM,
        compiler_params=pltpu.CompilerParams(vmem_limit_bytes=16 << 20),
        cost_estimate=pl.CostEstimate(flops=1000000, bytes_accessed=2 << 20, transcendentals=0),
    )(got)


def sim_kernel(xl_ref, xr_ref, out_ref, lx, rx):
    blocks, _, rows, _ = out_ref.shape
    rank, span = LANES, rows // 2
    for b in range(blocks):
        yl, core = b // CORES, b % CORES
        taken = pl.ds(yl * span, span)
        for i in range(2):
            put = pl.ds(b * rows + i * span, span)
            for half in range(2):
                near = (2 * half + i) * CORES + core
                lanes = slice(half * rank, (half + 1) * rank)
                lx[put, lanes] = xl_ref[near, taken]
                rx[put, lanes] = xr_ref[near, taken]
    for r in range(0, blocks, 2):
        right = rx[r * rows : (r + 2) * rows]
        for b in range(0, blocks, 2):
            sims = lax.dot_general(
                lx[b * rows : (b + 2) * rows], right, (((1,), (1,)), ((), ())), preferred_element_type=F32
            )
            for i in range(2):
                for j in range(2):
                    out_ref[b + i, r + j] = sims[i * rows : (i + 1) * rows, j * rows : (j + 1) * rows]


def sim_call(rows, left_x, right_x):
    operand = pltpu.VMEM((PARTS * rows, 2 * LANES), BF)
    return pl.pallas_call(
        sim_kernel,
        out_shape=jax.ShapeDtypeStruct((PARTS, PARTS, rows, rows), F32),
        in_specs=[VMEM, VMEM],
        out_specs=VMEM,
        scratch_shapes=[operand, operand],
        compiler_params=pltpu.CompilerParams(vmem_limit_bytes=24 << 20),
        cost_estimate=pl.CostEstimate(
            flops=4 * PARTS * PARTS * rows * rows * LANES, bytes_accessed=4 << 20, transcendentals=0
        ),
    )(left_x, right_x)


def sub_epoch_kernel(step_size, level, last, table_ref, mask_ref, sim_ref, *refs):
    if level == 0:
        all_ref, *refs = refs
    else:
        left_ref, right_ref, *refs = refs
    *outs, ls, lb, rs0, rb0, rs1, rb1, mf, kr, ks = refs
    blocks, rows, rank = ls.shape
    part, node = table_ref[INFO], table_ref[INFO + SUB + level]
    flip = jnp.int32(0) if level == 0 else table_ref[INFO + level]

    def place(slot):
        return slot if level == 0 else jnp.where(flip == 1, blocks - 1 - slot, slot)

    mf[...] = mask_ref[...].astype(F32)
    for b in range(blocks):
        row, lane = mask_place(node, b)
        kr[pl.ds(b, 1)] = mf[node // ZS % XS * CORES + b % CORES, pl.ds(row, 1)]
    values = kr[...]
    lanes = lax.broadcasted_iota(jnp.int32, values.shape, 1)
    for c in range(blocks):
        mine = jnp.where(lanes == lane + level * PARTS + c, values, 0.0)
        ks[c] = jnp.broadcast_to(jnp.sum(mine, axis=1, keepdims=True), values.shape)

    span = rows // 2
    for b in range(blocks):
        if level == 0:
            yl, core = b // CORES, b % CORES
            moved = pl.ds((YL + yl) * span, span)
            for i in range(2):
                put = pl.ds(i * span, span)
                left = all_ref[i * CORES + core, moved]
                right = all_ref[(2 + i) * CORES + core, moved]
                ls[b, put], rs0[b, put] = left.astype(F32), right.astype(F32)
                lb[b, put], rb0[b, put] = left, right
        else:
            left, right = left_ref[place(b)], right_ref[place(b)]
            ls[b], rs0[b] = left, right.astype(F32)
            lb[b], rb0[b] = left.astype(BF), right

    def cycle_step(step, source, target):
        (rs, rb), (rs_next, rb_next) = source, target
        preds = [
            lax.dot_general(lb[b], rb[b], (((1,), (1,)), ((), ())), preferred_element_type=F32)
            for b in range(blocks)
        ]
        resids = []
        for b in range(blocks):
            left, right = place(b), place(lax.rem(b + blocks - step, blocks))
            row = jnp.where(flip == 1, right, left)
            col = jnp.where(flip == 1, left, right)
            resids.append((ks[col, pl.ds(row, 1)] * (preds[b] - sim_ref[left, right])).astype(BF))
        grads_l = [jnp.dot(resids[b], rb[b], preferred_element_type=F32) for b in range(blocks)]
        grads_r = [
            lax.dot_general(resids[b], lb[b], (((0,), (0,)), ((), ())), preferred_element_type=F32)
            for b in range(blocks)
        ]
        for b in range(blocks):
            new_left = ls[b] - step_size * grads_l[b]
            ls[b] = new_left
            lb[b] = new_left.astype(BF)
        for b in range(blocks):
            new_right = rs[b] - step_size * grads_r[b]
            rs_next[(b + 1) % blocks] = new_right
            rb_next[(b + 1) % blocks] = new_right.astype(BF)

    def two_steps(pair, carry):
        cycle_step(2 * pair, (rs0, rb0), (rs1, rb1))
        cycle_step(2 * pair + 1, (rs1, rb1), (rs0, rb0))
        return carry

    lax.fori_loop(0, blocks // 2, two_steps, 0)
    if last:
        uo_ref, vo_ref = outs

        @pl.when(flip == 0)
        def _():
            uo_ref[...] = ls[place(part)]
            vo_ref[...] = rs0[place(part)]

        @pl.when(flip == 1)
        def _():
            uo_ref[...] = rs0[place(part)]
            vo_ref[...] = ls[place(part)]
    else:
        kept_ref, sent_ref = outs
        same = table_ref[INFO + 1 + level] == flip

        @pl.when(same)
        def _():
            for b in range(blocks):
                kept_ref[place(b)] = ls[b]
                sent_ref[place(b)] = lb[b]

        @pl.when(jnp.logical_not(same))
        def _():
            for b in range(blocks):
                kept_ref[place(b)] = rs0[b]
                sent_ref[place(b)] = rb0[b]


def sub_epoch_call(level, rows, table, mask, sims, *arrays):
    rank, last = LANES, level + 1 == SUB
    whole = (PARTS, rows, rank)
    if last:
        outs = (jax.ShapeDtypeStruct((rows, rank), F32),) * 2
    else:
        outs = (jax.ShapeDtypeStruct(whole, F32), jax.ShapeDtypeStruct(whole, BF))
    return pl.pallas_call(
        functools.partial(sub_epoch_kernel, 4.0 / rows, level, last),
        out_shape=outs,
        in_specs=[SMEM] + [VMEM] * (2 + len(arrays)),
        out_specs=(VMEM, VMEM),
        scratch_shapes=[pltpu.VMEM(whole, F32), pltpu.VMEM(whole, BF)] * 3
        + [
            pltpu.VMEM(mask.shape, F32),
            pltpu.VMEM((PARTS, LANES), F32),
            pltpu.VMEM((PARTS, PARTS, LANES), F32),
        ],
        compiler_params=pltpu.CompilerParams(vmem_limit_bytes=28 << 20),
        cost_estimate=pl.CostEstimate(
            flops=2 * PARTS * PARTS * rows * rows * 3 * rank,
            bytes_accessed=6 << 20,
            transcendentals=0,
        ),
    )(table, mask, sims, *arrays)


def swapped(array, stride):
    return lax.ppermute(array, BLK, [(i, i ^ stride) for i in range(PARTS)])


def spread(array, axes):
    return lax.all_to_all(array, axes, split_axis=0, concat_axis=0, tiled=True)


def local(features, factor_u, factor_v, tile_mask, matching):
    group = lax.axis_index(GRP).astype(jnp.int32)
    part = lax.axis_index(BLK).astype(jnp.int32)
    core = lax.axis_index("core")
    slot_rows, rank = factor_u.shape
    bits = [part // stride % 2 for stride in STRIDES]

    pieces = spread(pack_call(features, factor_u, factor_v).reshape(GROUPS, PIECE, rank), GRP)
    table = tables_call(jnp.stack([group, part]), matching, tile_mask)
    got = spread(pick_call(table, pieces), FAR)
    got = spread(regroup_call(got), NEAR).reshape(XS * CORES, -1, rank)
    half = YL * slot_rows // 2
    x0 = got[:, :half]
    mask = got[:, 2 * half :]

    def work(level, sims, *arrays):
        return sub_epoch_call(level, slot_rows, table, mask, sims, *arrays)

    left_x, coming_x = x0, swapped(x0, STRIDES[0])
    kept, sent = work(0, sim_call(slot_rows, got, got), got)
    for level in range(1, SUB):
        right = swapped(sent, STRIDES[level - 1])
        kept, coming_x = lax.optimization_barrier((kept, coming_x))
        right_x = coming_x
        if level > 1:
            other = swapped(coming_x, STRIDES[0])
            right_x = jnp.where(core == 0, jnp.concatenate([coming_x, other]), jnp.concatenate([other, coming_x]))
        sims = sim_call(slot_rows, left_x, right_x)
        if level + 1 < SUB:
            left_x = jnp.where(bits[level] == bits[level - 1], left_x, right_x)
            near = left_x.shape[0] // 2
            coming_x = swapped(lax.dynamic_slice_in_dim(left_x, core * near, near, 0), STRIDES[level])
        kept, sent = work(level, sims, kept, right)
    return kept, sent


def solution(mesh):
    fine = Mesh(mesh.devices.reshape(YH, XS, ZS, YL, CORES), ALL)
    in_specs = (P(ALL, None), P(ALL, None), P(ALL, None), P(ALL, None), P())
    out_specs = (P(ALL, None), P(ALL, None))
    return jax.shard_map(local, mesh=fine, in_specs=in_specs, out_specs=out_specs, check_vma=False)
```

```python
import functools

import jax
import jax.numpy as jnp
from jax import lax
from jax.experimental import pallas as pl
from jax.experimental.pallas import tpu as pltpu
from jax.sharding import Mesh, PartitionSpec as P

SUB = 4
GRP = ("yh", "x", "z")
BLK = ("yl", "core")
ALL = GRP + BLK
FAR = ("yh", "yl", "z")
NEAR = ("x", "core")
YH, XS, ZS, YL, CORES = 2, 4, 8, 4, 2
GROUPS, PARTS = YH * XS * ZS, YL * CORES
BF = jnp.bfloat16
F32 = jnp.float32
LANES = 128
PIECE = 8
STRIDES = (1, 2 * CORES, CORES)
INFO = GROUPS * PARTS
VALUES = INFO + 16
SMEM = pl.BlockSpec(memory_space=pltpu.SMEM)
VMEM = pl.BlockSpec(memory_space=pltpu.VMEM)


def pack_kernel(x_ref, u_ref, v_ref, out_ref):
    rows, rank = u_ref.shape
    out_ref[:rows] = x_ref[:, :rank].astype(BF)
    out_ref[rows : 2 * rows] = x_ref[:, rank:].astype(BF)
    out_ref[2 * rows : 3 * rows] = u_ref[...].astype(BF)
    out_ref[3 * rows :] = v_ref[...].astype(BF)


def pack_call(features, factor_u, factor_v):
    rows, rank = factor_u.shape
    return pl.pallas_call(
        pack_kernel,
        out_shape=jax.ShapeDtypeStruct((4 * rows, rank), BF),
        in_specs=[VMEM] * 3,
        out_specs=VMEM,
        cost_estimate=pl.CostEstimate(flops=100000, bytes_accessed=400000, transcendentals=0),
    )(features, factor_u, factor_v)


def mask_place(group, part):
    z = group % ZS
    return (group // (XS * ZS) * YL + part // CORES) * 2 + z // 4, (z % 4) * SUB * PARTS


def tables_kernel(here_ref, matching_ref, mask_ref, table_ref, inv_ref):
    group, part = here_ref[0], here_ref[1]

    def invert(e, carry):
        for t in range(SUB - 1):
            inv_ref[t * GROUPS + matching_ref[t, e]] = e
        return carry

    lax.fori_loop(0, GROUPS, invert, 0, unroll=4)

    def before(t, e):
        return inv_ref[t * GROUPS + e]

    def trace_back(d, carry):
        nodes = [d]
        for t in range(SUB - 2, -1, -1):
            nodes = [n for e in nodes for n in (e, before(t, e))]
        base = (d // (XS * ZS) * YL * ZS + d % ZS) * PARTS + d // ZS % XS * CORES
        for k in range(PARTS):
            yl, core = k // 2 % 2 * 2 + k // 4, k % 2
            table_ref[base + yl * ZS * PARTS + core] = nodes[k]
        return carry

    lax.fori_loop(0, GROUPS, trace_back, 0, unroll=2)

    table_ref[INFO] = part
    node = group
    for t in range(SUB - 1, -1, -1):
        table_ref[INFO + SUB + t] = node
        if t > 0:
            bit = part // STRIDES[t - 1] % 2
            table_ref[INFO + t] = bit
            node = jnp.where(bit == 1, before(t - 1, node), node)
    table_ref[INFO + 2 * SUB] = group
    for t in range(SUB):
        held = group
        for s in range(t - 1, -1, -1):
            held = before(s, held)
        for c in range(PARTS):
            table_ref[VALUES + t * PARTS + c] = mask_ref[0, held * PARTS + c]


def tables_call(here, matching, mask):
    return pl.pallas_call(
        tables_kernel,
        out_shape=jax.ShapeDtypeStruct((VALUES + SUB * PARTS,), jnp.int32),
        in_specs=[SMEM, SMEM, SMEM],
        out_specs=SMEM,
        scratch_shapes=[pltpu.SMEM((GROUPS * (SUB - 1),), jnp.int32)],
        cost_estimate=pl.CostEstimate(flops=2000000, bytes_accessed=4096, transcendentals=0),
    )(here, matching, mask)


def pick_kernel(table_ref, pieces_ref, out_ref):
    row, lane = mask_place(table_ref[INFO + 2 * SUB], table_ref[INFO])
    lanes = lax.broadcasted_iota(jnp.int32, (PIECE, LANES), 1)
    values = jnp.zeros((PIECE, LANES), jnp.int32)
    for i in range(SUB * PARTS):
        values = jnp.where(lanes == lane + i, table_ref[VALUES + i], values)
    rows = lax.broadcasted_iota(jnp.int32, (PIECE, LANES), 0)
    tile = jnp.where(rows == row % PIECE, values, 0).astype(F32).astype(BF)

    def one(far, carry):
        for near in range(XS * CORES):
            out_ref[far, near] = pieces_ref[table_ref[far * XS * CORES + near]]
        out_ref[far, XS * CORES] = tile
        return carry

    lax.fori_loop(0, out_ref.shape[0], one, 0, unroll=4)


def pick_call(table, pieces):
    return pl.pallas_call(
        pick_kernel,
        out_shape=jax.ShapeDtypeStruct((YH * YL * ZS, XS * CORES + 1, PIECE, LANES), BF),
        in_specs=[SMEM, VMEM],
        out_specs=VMEM,
        compiler_params=pltpu.CompilerParams(vmem_limit_bytes=16 << 20),
        cost_estimate=pl.CostEstimate(flops=1000000, bytes_accessed=2 << 20, transcendentals=0),
    )(table, pieces)


def regroup_kernel(got_ref, x_ref, uv_ref):
    half = YL * ZS
    for near in range(XS * CORES):
        x_ref[near] = got_ref[:half, near]
        uv_ref[near, :half] = got_ref[half:, near]
    for yh in range(YH):
        total = jnp.sum(got_ref[yh * half : (yh + 1) * half, XS * CORES].astype(F32), axis=0).astype(BF)
        for near in range(XS * CORES):
            uv_ref[near, half + yh] = total


def regroup_call(got):
    half = YL * ZS
    return pl.pallas_call(
        regroup_kernel,
        out_shape=(
            jax.ShapeDtypeStruct((XS * CORES, half, PIECE, LANES), BF),
            jax.ShapeDtypeStruct((XS * CORES, half + YH, PIECE, LANES), BF),
        ),
        in_specs=[VMEM],
        out_specs=(VMEM, VMEM),
        compiler_params=pltpu.CompilerParams(vmem_limit_bytes=16 << 20),
        cost_estimate=pl.CostEstimate(flops=1000000, bytes_accessed=2 << 20, transcendentals=0),
    )(got)


def sim_kernel(xl_ref, xr_ref, out_ref, lx, rx):
    blocks, _, rows, _ = out_ref.shape
    rank, span = LANES, rows // 2
    for b in range(blocks):
        yl, core = b // CORES, b % CORES
        taken = pl.ds(yl * span, span)
        for i in range(2):
            put = pl.ds(b * rows + i * span, span)
            for half in range(2):
                near = (2 * half + i) * CORES + core
                lanes = slice(half * rank, (half + 1) * rank)
                lx[put, lanes] = xl_ref[near, taken]
                rx[put, lanes] = xr_ref[near, taken]
    for r in range(0, blocks, 2):
        right = rx[r * rows : (r + 2) * rows]
        for b in range(0, blocks, 2):
            sims = lax.dot_general(
                lx[b * rows : (b + 2) * rows], right, (((1,), (1,)), ((), ())), preferred_element_type=F32
            )
            for i in range(2):
                for j in range(2):
                    out_ref[b + i, r + j] = sims[i * rows : (i + 1) * rows, j * rows : (j + 1) * rows]


def sim_call(rows, left_x, right_x):
    operand = pltpu.VMEM((PARTS * rows, 2 * LANES), BF)
    return pl.pallas_call(
        sim_kernel,
        out_shape=jax.ShapeDtypeStruct((PARTS, PARTS, rows, rows), F32),
        in_specs=[VMEM, VMEM],
        out_specs=VMEM,
        scratch_shapes=[operand, operand],
        compiler_params=pltpu.CompilerParams(vmem_limit_bytes=24 << 20),
        cost_estimate=pl.CostEstimate(
            flops=4 * PARTS * PARTS * rows * rows * LANES, bytes_accessed=4 << 20, transcendentals=0
        ),
    )(left_x, right_x)


def sub_epoch_kernel(step_size, level, last, table_ref, mask_ref, sim_ref, *refs):
    if level == 0:
        all_ref, *refs = refs
    else:
        left_ref, right_ref, *refs = refs
    *outs, ls, lb, rs0, rb0, rs1, rb1, mf, kr, ks = refs
    blocks, rows, rank = ls.shape
    part, node = table_ref[INFO], table_ref[INFO + SUB + level]
    flip = jnp.int32(0) if level == 0 else table_ref[INFO + level]

    def place(slot):
        return slot if level == 0 else jnp.where(flip == 1, blocks - 1 - slot, slot)

    mf[...] = mask_ref[...].astype(F32)
    for b in range(blocks):
        row, lane = mask_place(node, b)
        kr[pl.ds(b, 1)] = mf[node // ZS % XS * CORES + b % CORES, pl.ds(row, 1)]
    values = kr[...]
    lanes = lax.broadcasted_iota(jnp.int32, values.shape, 1)
    for c in range(blocks):
        mine = jnp.where(lanes == lane + level * PARTS + c, values, 0.0)
        ks[c] = jnp.broadcast_to(jnp.sum(mine, axis=1, keepdims=True), values.shape)

    span = rows // 2
    for b in range(blocks):
        if level == 0:
            yl, core = b // CORES, b % CORES
            moved = pl.ds(yl * span, span)
            for i in range(2):
                put = pl.ds(i * span, span)
                left = all_ref[i * CORES + core, moved]
                right = all_ref[(2 + i) * CORES + core, moved]
                ls[b, put], rs0[b, put] = left.astype(F32), right.astype(F32)
                lb[b, put], rb0[b, put] = left, right
        else:
            left, right = left_ref[place(b)], right_ref[place(b)]
            ls[b], rs0[b] = left, right.astype(F32)
            lb[b], rb0[b] = left.astype(BF), right

    def cycle_step(step, source, target, spots):
        (rs, rb), (rs_next, rb_next) = source, target
        preds = [
            lax.dot_general(lb[b], rb[b], (((1,), (1,)), ((), ())), preferred_element_type=F32) for b in spots
        ]
        resids = []
        for b, pred in zip(spots, preds):
            left, right = place(b), place(lax.rem(b + blocks - step, blocks))
            row = jnp.where(flip == 1, right, left)
            col = jnp.where(flip == 1, left, right)
            resids.append((ks[col, pl.ds(row, 1)] * (pred - sim_ref[left, right])).astype(BF))
        grads_l = [jnp.dot(resid, rb[b], preferred_element_type=F32) for b, resid in zip(spots, resids)]
        grads_r = [
            lax.dot_general(resid, lb[b], (((0,), (0,)), ((), ())), preferred_element_type=F32)
            for b, resid in zip(spots, resids)
        ]
        for b, grad in zip(spots, grads_l):
            new_left = ls[b] - step_size * grad
            ls[b] = new_left
            lb[b] = new_left.astype(BF)
        for b, grad in zip(spots, grads_r):
            new_right = rs[b] - step_size * grad
            after = (b + 1) % blocks if isinstance(b, int) else lax.rem(b + 1, blocks)
            rs_next[after] = new_right
            rb_next[after] = new_right.astype(BF)

    turns = ((rs0, rb0), (rs1, rb1))
    every = list(range(blocks))
    if last:
        for step in range(blocks):
            count = blocks + 1 - step
            mine = [lax.rem(place(part) + blocks - i, blocks) for i in range(count)]
            cycle_step(step, turns[step % 2], turns[1 - step % 2], every if count >= blocks else mine)
    else:

        def two_steps(pair, carry):
            cycle_step(2 * pair, *turns, every)
            cycle_step(2 * pair + 1, *turns[::-1], every)
            return carry

        lax.fori_loop(0, blocks // 2, two_steps, 0)
    if last:
        uo_ref, vo_ref = outs

        @pl.when(flip == 0)
        def _():
            uo_ref[...] = ls[place(part)]
            vo_ref[...] = rs0[place(part)]

        @pl.when(flip == 1)
        def _():
            uo_ref[...] = rs0[place(part)]
            vo_ref[...] = ls[place(part)]
    else:
        kept_ref, sent_ref = outs
        same = table_ref[INFO + 1 + level] == flip

        @pl.when(same)
        def _():
            for b in range(blocks):
                kept_ref[place(b)] = ls[b]
                sent_ref[place(b)] = lb[b]

        @pl.when(jnp.logical_not(same))
        def _():
            for b in range(blocks):
                kept_ref[place(b)] = rs0[b]
                sent_ref[place(b)] = rb0[b]


def sub_epoch_call(level, rows, table, mask, sims, *arrays):
    rank, last = LANES, level + 1 == SUB
    whole = (PARTS, rows, rank)
    if last:
        outs = (jax.ShapeDtypeStruct((rows, rank), F32),) * 2
    else:
        outs = (jax.ShapeDtypeStruct(whole, F32), jax.ShapeDtypeStruct(whole, BF))
    return pl.pallas_call(
        functools.partial(sub_epoch_kernel, 4.0 / rows, level, last),
        out_shape=outs,
        in_specs=[SMEM] + [VMEM] * (2 + len(arrays)),
        out_specs=(VMEM, VMEM),
        scratch_shapes=[pltpu.VMEM(whole, F32), pltpu.VMEM(whole, BF)] * 3
        + [
            pltpu.VMEM(mask.shape, F32),
            pltpu.VMEM((PARTS, LANES), F32),
            pltpu.VMEM((PARTS, PARTS, LANES), F32),
        ],
        compiler_params=pltpu.CompilerParams(vmem_limit_bytes=28 << 20),
        cost_estimate=pl.CostEstimate(
            flops=2 * PARTS * PARTS * rows * rows * 3 * rank,
            bytes_accessed=6 << 20,
            transcendentals=0,
        ),
    )(table, mask, sims, *arrays)


def swapped(array, stride):
    return lax.ppermute(array, BLK, [(i, i ^ stride) for i in range(PARTS)])


def spread(array, axes):
    return lax.all_to_all(array, axes, split_axis=0, concat_axis=0, tiled=True)


def local(features, factor_u, factor_v, tile_mask, matching):
    group = lax.axis_index(GRP).astype(jnp.int32)
    part = lax.axis_index(BLK).astype(jnp.int32)
    core = lax.axis_index("core")
    slot_rows, rank = factor_u.shape
    bits = [part // stride % 2 for stride in STRIDES]

    pieces = spread(pack_call(features, factor_u, factor_v).reshape(GROUPS, PIECE, rank), GRP)
    table = tables_call(jnp.stack([group, part]), matching, tile_mask)
    got = spread(pick_call(table, pieces), FAR)
    x0, uv = regroup_call(got)
    x0 = spread(x0, NEAR).reshape(XS * CORES, -1, rank)
    uv = spread(uv, NEAR).reshape(XS * CORES, -1, rank)
    mask = uv[:, x0.shape[1] :]

    def work(level, sims, *arrays):
        return sub_epoch_call(level, slot_rows, table, mask, sims, *arrays)

    def joined(first):
        second = swapped(first, STRIDES[0])
        return jnp.where(core == 0, jnp.concatenate([first, second]), jnp.concatenate([second, first]))

    def half_of(x):
        return lax.dynamic_slice_in_dim(x, core * (XS * CORES // 2), XS * CORES // 2, 0)

    y0 = swapped(x0, STRIDES[0])
    sims = sim_call(slot_rows, x0, x0)
    x1 = jnp.where(bits[1] == bits[0], x0, y0)
    first = swapped(half_of(x1), STRIDES[1])
    sims_next = sim_call(slot_rows, x0, y0)
    kept, sent = work(0, sims, uv)
    right = swapped(sent, STRIDES[0])
    kept, first = lax.optimization_barrier((kept, first))
    y1 = joined(first)
    x2 = jnp.where(bits[2] == bits[1], x1, y1)
    first = swapped(half_of(x2), STRIDES[2])
    kept, sent = work(1, sims_next, kept, right)
    right = swapped(sent, STRIDES[1])
    sims = sim_call(slot_rows, x1, y1)
    kept, sent = work(2, sims, kept, right)
    right = swapped(sent, STRIDES[2])
    kept, first = lax.optimization_barrier((kept, first))
    return work(3, sim_call(slot_rows, x2, joined(first)), kept, right)


def solution(mesh):
    fine = Mesh(mesh.devices.reshape(YH, XS, ZS, YL, CORES), ALL)
    in_specs = (P(ALL, None), P(ALL, None), P(ALL, None), P(ALL, None), P())
    out_specs = (P(ALL, None), P(ALL, None))
    return jax.shard_map(local, mesh=fine, in_specs=in_specs, out_specs=out_specs, check_vma=False)
```

```python
import functools

import jax
import jax.numpy as jnp
from jax import lax
from jax.experimental import pallas as pl
from jax.experimental.pallas import tpu as pltpu
from jax.sharding import Mesh, PartitionSpec as P

SUB = 4
GRP = ("yh", "x", "z")
BLK = ("yl", "core")
ALL = GRP + BLK
FAR = ("yh", "yl", "z")
NEAR = ("x", "core")
YH, XS, ZS, YL, CORES = 2, 4, 8, 4, 2
GROUPS, PARTS = YH * XS * ZS, YL * CORES
BF = jnp.bfloat16
F32 = jnp.float32
LANES = 128
PIECE = 8
STRIDES = (1, 2 * CORES, CORES)
INFO = GROUPS * PARTS
VALUES = INFO + 16
SMEM = pl.BlockSpec(memory_space=pltpu.SMEM)
VMEM = pl.BlockSpec(memory_space=pltpu.VMEM)


def pack_kernel(x_ref, u_ref, v_ref, out_ref):
    rows, rank = u_ref.shape
    out_ref[:rows] = x_ref[:, :rank].astype(BF)
    out_ref[rows : 2 * rows] = x_ref[:, rank:].astype(BF)
    out_ref[2 * rows : 3 * rows] = u_ref[...].astype(BF)
    out_ref[3 * rows :] = v_ref[...].astype(BF)


def pack_call(features, factor_u, factor_v):
    rows, rank = factor_u.shape
    return pl.pallas_call(
        pack_kernel,
        out_shape=jax.ShapeDtypeStruct((4 * rows, rank), BF),
        in_specs=[VMEM] * 3,
        out_specs=VMEM,
        cost_estimate=pl.CostEstimate(flops=100000, bytes_accessed=400000, transcendentals=0),
    )(features, factor_u, factor_v)


def mask_place(group, part):
    z = group % ZS
    return (group // (XS * ZS) * YL + part // CORES) * 2 + z // 4, (z % 4) * SUB * PARTS


def tables_kernel(here_ref, matching_ref, mask_ref, table_ref, inv_ref):
    group, part = here_ref[0], here_ref[1]

    def invert(e, carry):
        for t in range(SUB - 1):
            inv_ref[t * GROUPS + matching_ref[t, e]] = e
        return carry

    lax.fori_loop(0, GROUPS, invert, 0, unroll=4)

    def before(t, e):
        return inv_ref[t * GROUPS + e]

    def trace_back(d, carry):
        nodes = [d]
        for t in range(SUB - 2, -1, -1):
            nodes = [n for e in nodes for n in (e, before(t, e))]
        base = (d // (XS * ZS) * YL * ZS + d % ZS) * PARTS + d // ZS % XS * CORES
        for k in range(PARTS):
            yl, core = k // 2 % 2 * 2 + k // 4, k % 2
            table_ref[base + yl * ZS * PARTS + core] = nodes[k]
        return carry

    lax.fori_loop(0, GROUPS, trace_back, 0, unroll=2)

    table_ref[INFO] = part
    node = group
    for t in range(SUB - 1, -1, -1):
        table_ref[INFO + SUB + t] = node
        if t > 0:
            bit = part // STRIDES[t - 1] % 2
            table_ref[INFO + t] = bit
            node = jnp.where(bit == 1, before(t - 1, node), node)
    table_ref[INFO + 2 * SUB] = group
    for t in range(SUB):
        held = group
        for s in range(t - 1, -1, -1):
            held = before(s, held)
        for c in range(PARTS):
            table_ref[VALUES + t * PARTS + c] = mask_ref[0, held * PARTS + c]


def tables_call(here, matching, mask):
    return pl.pallas_call(
        tables_kernel,
        out_shape=jax.ShapeDtypeStruct((VALUES + SUB * PARTS,), jnp.int32),
        in_specs=[SMEM, SMEM, SMEM],
        out_specs=SMEM,
        scratch_shapes=[pltpu.SMEM((GROUPS * (SUB - 1),), jnp.int32)],
        cost_estimate=pl.CostEstimate(flops=2000000, bytes_accessed=4096, transcendentals=0),
    )(here, matching, mask)


def pick_kernel(table_ref, pieces_ref, out_ref):
    row, lane = mask_place(table_ref[INFO + 2 * SUB], table_ref[INFO])
    lanes = lax.broadcasted_iota(jnp.int32, (PIECE, LANES), 1)
    values = jnp.zeros((PIECE, LANES), jnp.int32)
    for i in range(SUB * PARTS):
        values = jnp.where(lanes == lane + i, table_ref[VALUES + i], values)
    rows = lax.broadcasted_iota(jnp.int32, (PIECE, LANES), 0)
    tile = jnp.where(rows == row % PIECE, values, 0).astype(F32).astype(BF)

    def one(far, carry):
        for near in range(XS * CORES):
            out_ref[far, near] = pieces_ref[table_ref[far * XS * CORES + near]]
        out_ref[far, XS * CORES] = tile
        return carry

    lax.fori_loop(0, out_ref.shape[0], one, 0, unroll=4)


def pick_call(table, pieces):
    return pl.pallas_call(
        pick_kernel,
        out_shape=jax.ShapeDtypeStruct((YH * YL * ZS, XS * CORES + 1, PIECE, LANES), BF),
        in_specs=[SMEM, VMEM],
        out_specs=VMEM,
        compiler_params=pltpu.CompilerParams(vmem_limit_bytes=16 << 20),
        cost_estimate=pl.CostEstimate(flops=1000000, bytes_accessed=2 << 20, transcendentals=0),
    )(table, pieces)


def regroup_kernel(got_ref, out_ref):
    far = YH * YL * ZS
    for near in range(XS * CORES):
        out_ref[near, :far] = got_ref[:, near]
    for yh in range(YH):
        span = far // YH
        total = jnp.sum(got_ref[yh * span : (yh + 1) * span, XS * CORES].astype(F32), axis=0).astype(BF)
        for near in range(XS * CORES):
            out_ref[near, far + yh] = total


def regroup_call(got):
    return pl.pallas_call(
        regroup_kernel,
        out_shape=jax.ShapeDtypeStruct((XS * CORES, YH * YL * ZS + YH, PIECE, LANES), BF),
        in_specs=[VMEM],
        out_specs=VMEM,
        compiler_params=pltpu.CompilerParams(vmem_limit_bytes=16 << 20),
        cost_estimate=pl.CostEstimate(flops=1000000, bytes_accessed=2 << 20, transcendentals=0),
    )(got)


def sim_kernel(xl_ref, xr_ref, out_ref, lx, rx):
    blocks, _, rows, _ = out_ref.shape
    rank, span = LANES, rows // 2
    for b in range(blocks):
        yl, core = b // CORES, b % CORES
        taken = pl.ds(yl * span, span)
        for i in range(2):
            put = pl.ds(b * rows + i * span, span)
            for half in range(2):
                near = (2 * half + i) * CORES + core
                lanes = slice(half * rank, (half + 1) * rank)
                lx[put, lanes] = xl_ref[near, taken]
                rx[put, lanes] = xr_ref[near, taken]
    for r in range(0, blocks, 2):
        right = rx[r * rows : (r + 2) * rows]
        for b in range(0, blocks, 2):
            sims = lax.dot_general(
                lx[b * rows : (b + 2) * rows], right, (((1,), (1,)), ((), ())), preferred_element_type=F32
            )
            for i in range(2):
                for j in range(2):
                    out_ref[b + i, r + j] = sims[i * rows : (i + 1) * rows, j * rows : (j + 1) * rows]


def sim_call(rows, left_x, right_x):
    operand = pltpu.VMEM((PARTS * rows, 2 * LANES), BF)
    return pl.pallas_call(
        sim_kernel,
        out_shape=jax.ShapeDtypeStruct((PARTS, PARTS, rows, rows), F32),
        in_specs=[VMEM, VMEM],
        out_specs=VMEM,
        scratch_shapes=[operand, operand],
        compiler_params=pltpu.CompilerParams(vmem_limit_bytes=24 << 20),
        cost_estimate=pl.CostEstimate(
            flops=4 * PARTS * PARTS * rows * rows * LANES, bytes_accessed=4 << 20, transcendentals=0
        ),
    )(left_x, right_x)


def sub_epoch_kernel(step_size, level, last, table_ref, mask_ref, sim_ref, *refs):
    if level == 0:
        all_ref, *refs = refs
    else:
        left_ref, right_ref, *refs = refs
    *outs, ls, lb, rs0, rb0, rs1, rb1, mf, kr, ks = refs
    blocks, rows, rank = ls.shape
    part, node = table_ref[INFO], table_ref[INFO + SUB + level]
    flip = jnp.int32(0) if level == 0 else table_ref[INFO + level]

    def place(slot):
        return slot if level == 0 else jnp.where(flip == 1, blocks - 1 - slot, slot)

    mf[...] = mask_ref[...].astype(F32)
    for b in range(blocks):
        row, lane = mask_place(node, b)
        kr[pl.ds(b, 1)] = mf[node // ZS % XS * CORES + b % CORES, pl.ds(row, 1)]
    values = kr[...]
    lanes = lax.broadcasted_iota(jnp.int32, values.shape, 1)
    for c in range(blocks):
        mine = jnp.where(lanes == lane + level * PARTS + c, values, 0.0)
        ks[c] = jnp.broadcast_to(step_size * jnp.sum(mine, axis=1, keepdims=True), values.shape)

    span = rows // 2
    for b in range(blocks):
        if level == 0:
            yl, core = b // CORES, b % CORES
            moved = pl.ds((YL + yl) * span, span)
            for i in range(2):
                put = pl.ds(i * span, span)
                left = all_ref[i * CORES + core, moved]
                right = all_ref[(2 + i) * CORES + core, moved]
                ls[b, put], rs0[b, put] = left.astype(F32), right.astype(F32)
                lb[b, put], rb0[b, put] = left, right
        else:
            left, right = left_ref[place(b)], right_ref[place(b)]
            ls[b], rs0[b] = left, right.astype(F32)
            lb[b], rb0[b] = left.astype(BF), right

    def cycle_step(step, source, target, spots):
        (rs, rb), (rs_next, rb_next) = source, target
        preds = [
            lax.dot_general(lb[b], rb[b], (((1,), (1,)), ((), ())), preferred_element_type=F32) for b in spots
        ]
        resids = []
        for b, pred in zip(spots, preds):
            left, right = place(b), place(lax.rem(b + blocks - step, blocks))
            row = jnp.where(flip == 1, right, left)
            col = jnp.where(flip == 1, left, right)
            resids.append((ks[col, pl.ds(row, 1)] * (pred - sim_ref[left, right])).astype(BF))
        grads_l = [jnp.dot(resid, rb[b], preferred_element_type=F32) for b, resid in zip(spots, resids)]
        grads_r = [
            lax.dot_general(resid, lb[b], (((0,), (0,)), ((), ())), preferred_element_type=F32)
            for b, resid in zip(spots, resids)
        ]
        for b, grad in zip(spots, grads_l):
            new_left = ls[b] - grad
            ls[b] = new_left
            lb[b] = new_left.astype(BF)
        for b, grad in zip(spots, grads_r):
            new_right = rs[b] - grad
            after = (b + 1) % blocks if isinstance(b, int) else lax.rem(b + 1, blocks)
            rs_next[after] = new_right
            rb_next[after] = new_right.astype(BF)

    turns = ((rs0, rb0), (rs1, rb1))
    every = list(range(blocks))
    if last:
        for step in range(blocks):
            count = blocks + 1 - step
            mine = [lax.rem(place(part) + blocks - i, blocks) for i in range(count)]
            cycle_step(step, turns[step % 2], turns[1 - step % 2], every if count >= blocks else mine)
    else:

        def two_steps(pair, carry):
            cycle_step(2 * pair, *turns, every)
            cycle_step(2 * pair + 1, *turns[::-1], every)
            return carry

        lax.fori_loop(0, blocks // 2, two_steps, 0)
    if last:
        uo_ref, vo_ref = outs

        @pl.when(flip == 0)
        def _():
            uo_ref[...] = ls[place(part)]
            vo_ref[...] = rs0[place(part)]

        @pl.when(flip == 1)
        def _():
            uo_ref[...] = rs0[place(part)]
            vo_ref[...] = ls[place(part)]
    else:
        kept_ref, sent_ref = outs
        same = table_ref[INFO + 1 + level] == flip

        @pl.when(same)
        def _():
            for b in range(blocks):
                kept_ref[place(b)] = ls[b]
                sent_ref[place(b)] = lb[b]

        @pl.when(jnp.logical_not(same))
        def _():
            for b in range(blocks):
                kept_ref[place(b)] = rs0[b]
                sent_ref[place(b)] = rb0[b]


def sub_epoch_call(level, rows, table, mask, sims, *arrays):
    rank, last = LANES, level + 1 == SUB
    whole = (PARTS, rows, rank)
    if last:
        outs = (jax.ShapeDtypeStruct((rows, rank), F32),) * 2
    else:
        outs = (jax.ShapeDtypeStruct(whole, F32), jax.ShapeDtypeStruct(whole, BF))
    return pl.pallas_call(
        functools.partial(sub_epoch_kernel, 4.0 / rows, level, last),
        out_shape=outs,
        in_specs=[SMEM] + [VMEM] * (2 + len(arrays)),
        out_specs=(VMEM, VMEM),
        scratch_shapes=[pltpu.VMEM(whole, F32), pltpu.VMEM(whole, BF)] * 3
        + [
            pltpu.VMEM(mask.shape, F32),
            pltpu.VMEM((PARTS, LANES), F32),
            pltpu.VMEM((PARTS, PARTS, LANES), F32),
        ],
        compiler_params=pltpu.CompilerParams(vmem_limit_bytes=28 << 20),
        cost_estimate=pl.CostEstimate(
            flops=2 * PARTS * PARTS * rows * rows * 3 * rank,
            bytes_accessed=6 << 20,
            transcendentals=0,
        ),
    )(table, mask, sims, *arrays)


def swapped(array, stride):
    return lax.ppermute(array, BLK, [(i, i ^ stride) for i in range(PARTS)])


def spread(array, axes):
    return lax.all_to_all(array, axes, split_axis=0, concat_axis=0, tiled=True)


def local(features, factor_u, factor_v, tile_mask, matching):
    group = lax.axis_index(GRP).astype(jnp.int32)
    part = lax.axis_index(BLK).astype(jnp.int32)
    core = lax.axis_index("core")
    slot_rows, rank = factor_u.shape
    bits = [part // stride % 2 for stride in STRIDES]

    pieces = spread(pack_call(features, factor_u, factor_v).reshape(GROUPS, PIECE, rank), GRP)
    table = tables_call(jnp.stack([group, part]), matching, tile_mask)
    got = spread(pick_call(table, pieces), FAR)
    got = spread(regroup_call(got), NEAR).reshape(XS * CORES, -1, rank)
    half = YL * slot_rows // 2
    x0, mask = got[:, :half], got[:, 2 * half :]

    def work(level, sims, *arrays):
        return sub_epoch_call(level, slot_rows, table, mask, sims, *arrays)

    def joined(first):
        second = swapped(first, STRIDES[0])
        return jnp.where(core == 0, jnp.concatenate([first, second]), jnp.concatenate([second, first]))

    def half_of(x):
        return lax.dynamic_slice_in_dim(x, core * (XS * CORES // 2), XS * CORES // 2, 0)

    away, next_bit = STRIDES[1], [b // STRIDES[1] % 2 for b in range(PARTS)]
    first = lax.ppermute(x0, BLK, [(b, b ^ away) for b in range(PARTS) if b % CORES == next_bit[b]])
    y0 = swapped(x0, STRIDES[0])
    sims = sim_call(slot_rows, got, got)
    x1 = jnp.where(bits[1] == bits[0], x0, y0)
    kept, sent = work(0, sims, got)
    right = swapped(sent, STRIDES[0])
    sims = sim_call(slot_rows, x0, y0)
    right, first = lax.optimization_barrier((right, first))
    second = lax.ppermute(first, BLK, [(b, b ^ STRIDES[0]) for b in range(PARTS) if b % CORES != next_bit[b]])
    kept, sent = work(1, sims, kept, right)
    right = swapped(sent, STRIDES[1])
    y1 = jnp.where(bits[0] == bits[1], second, first)
    sims = sim_call(slot_rows, x1, y1)
    x2 = jnp.where(bits[2] == bits[1], x1, y1)
    first = swapped(half_of(x2), STRIDES[2])
    kept, sent = work(2, sims, kept, right)
    right = swapped(sent, STRIDES[2])
    kept, first = lax.optimization_barrier((kept, first))
    return work(3, sim_call(slot_rows, x2, joined(first)), kept, right)


def solution(mesh):
    fine = Mesh(mesh.devices.reshape(YH, XS, ZS, YL, CORES), ALL)
    in_specs = (P(ALL, None), P(ALL, None), P(ALL, None), P(ALL, None), P())
    out_specs = (P(ALL, None), P(ALL, None))
    return jax.shard_map(local, mesh=fine, in_specs=in_specs, out_specs=out_specs, check_vma=False)
```

```python
import functools

import jax
import jax.numpy as jnp
from jax import lax
from jax.experimental import pallas as pl
from jax.experimental.pallas import tpu as pltpu
from jax.sharding import Mesh, PartitionSpec as P

SUB = 4
GRP = ("yh", "x", "z")
BLK = ("yl", "core")
ALL = GRP + BLK
FAR = ("yh", "yl", "z")
NEAR = ("x", "core")
YH, XS, ZS, YL, CORES = 2, 4, 8, 4, 2
GROUPS, PARTS = YH * XS * ZS, YL * CORES
BF = jnp.bfloat16
F32 = jnp.float32
LANES = 128
PIECE = 8
STRIDES = (1, 2 * CORES, CORES)
INFO = GROUPS * PARTS
VALUES = INFO + 16
SMEM = pl.BlockSpec(memory_space=pltpu.SMEM)
VMEM = pl.BlockSpec(memory_space=pltpu.VMEM)


def pack_kernel(x_ref, u_ref, v_ref, out_ref):
    rows, rank = u_ref.shape
    out_ref[:rows] = x_ref[:, :rank].astype(BF)
    out_ref[rows : 2 * rows] = x_ref[:, rank:].astype(BF)
    out_ref[2 * rows : 3 * rows] = u_ref[...].astype(BF)
    out_ref[3 * rows :] = v_ref[...].astype(BF)


def pack_call(features, factor_u, factor_v):
    rows, rank = factor_u.shape
    return pl.pallas_call(
        pack_kernel,
        out_shape=jax.ShapeDtypeStruct((4 * rows, rank), BF),
        in_specs=[VMEM] * 3,
        out_specs=VMEM,
        cost_estimate=pl.CostEstimate(flops=100000, bytes_accessed=400000, transcendentals=0),
    )(features, factor_u, factor_v)


def mask_place(group, part):
    z = group % ZS
    return (group // (XS * ZS) * YL + part // CORES) * 2 + z // 4, (z % 4) * SUB * PARTS


def tables_kernel(here_ref, matching_ref, mask_ref, table_ref, inv_ref):
    group, part = here_ref[0], here_ref[1]

    def invert(e, carry):
        for t in range(SUB - 1):
            inv_ref[t * GROUPS + matching_ref[t, e]] = e
        return carry

    lax.fori_loop(0, GROUPS, invert, 0, unroll=4)

    def before(t, e):
        return inv_ref[t * GROUPS + e]

    def trace_back(d, carry):
        nodes = [d]
        for t in range(SUB - 2, -1, -1):
            nodes = [n for e in nodes for n in (e, before(t, e))]
        base = (d // (XS * ZS) * YL * ZS + d % ZS) * PARTS + d // ZS % XS * CORES
        for k in range(PARTS):
            yl, core = k // 2 % 2 * 2 + k // 4, k % 2
            table_ref[base + yl * ZS * PARTS + core] = nodes[k]
        return carry

    lax.fori_loop(0, GROUPS, trace_back, 0, unroll=2)

    table_ref[INFO] = part
    node = group
    for t in range(SUB - 1, -1, -1):
        table_ref[INFO + SUB + t] = node
        if t > 0:
            bit = part // STRIDES[t - 1] % 2
            table_ref[INFO + t] = bit
            node = jnp.where(bit == 1, before(t - 1, node), node)
    table_ref[INFO + 2 * SUB] = group
    for t in range(SUB):
        held = group
        for s in range(t - 1, -1, -1):
            held = before(s, held)
        for c in range(PARTS):
            table_ref[VALUES + t * PARTS + c] = mask_ref[0, held * PARTS + c]


def tables_call(here, matching, mask):
    return pl.pallas_call(
        tables_kernel,
        out_shape=jax.ShapeDtypeStruct((VALUES + SUB * PARTS,), jnp.int32),
        in_specs=[SMEM, SMEM, SMEM],
        out_specs=SMEM,
        scratch_shapes=[pltpu.SMEM((GROUPS * (SUB - 1),), jnp.int32)],
        cost_estimate=pl.CostEstimate(flops=2000000, bytes_accessed=4096, transcendentals=0),
    )(here, matching, mask)


def pick_kernel(table_ref, pieces_ref, out_ref):
    row, lane = mask_place(table_ref[INFO + 2 * SUB], table_ref[INFO])
    lanes = lax.broadcasted_iota(jnp.int32, (PIECE, LANES), 1)
    values = jnp.zeros((PIECE, LANES), jnp.int32)
    for i in range(SUB * PARTS):
        values = jnp.where(lanes == lane + i, table_ref[VALUES + i], values)
    rows = lax.broadcasted_iota(jnp.int32, (PIECE, LANES), 0)
    tile = jnp.where(rows == row % PIECE, values, 0).astype(F32).astype(BF)

    def one(far, carry):
        for near in range(XS * CORES):
            out_ref[far, near] = pieces_ref[table_ref[far * XS * CORES + near]]
        out_ref[far, XS * CORES] = tile
        return carry

    lax.fori_loop(0, out_ref.shape[0], one, 0, unroll=4)


def pick_call(table, pieces):
    return pl.pallas_call(
        pick_kernel,
        out_shape=jax.ShapeDtypeStruct((YH * YL * ZS, XS * CORES + 1, PIECE, LANES), BF),
        in_specs=[SMEM, VMEM],
        out_specs=VMEM,
        compiler_params=pltpu.CompilerParams(vmem_limit_bytes=16 << 20),
        cost_estimate=pl.CostEstimate(flops=1000000, bytes_accessed=2 << 20, transcendentals=0),
    )(table, pieces)


def regroup_kernel(got_ref, out_ref):
    far = YH * YL * ZS
    for near in range(XS * CORES):
        out_ref[near, :far] = got_ref[:, near]
    for yh in range(YH):
        span = far // YH
        total = jnp.sum(got_ref[yh * span : (yh + 1) * span, XS * CORES].astype(F32), axis=0).astype(BF)
        for near in range(XS * CORES):
            out_ref[near, far + yh] = total


def regroup_call(got):
    return pl.pallas_call(
        regroup_kernel,
        out_shape=jax.ShapeDtypeStruct((XS * CORES, YH * YL * ZS + YH, PIECE, LANES), BF),
        in_specs=[VMEM],
        out_specs=VMEM,
        compiler_params=pltpu.CompilerParams(vmem_limit_bytes=16 << 20),
        cost_estimate=pl.CostEstimate(flops=1000000, bytes_accessed=2 << 20, transcendentals=0),
    )(got)


def sim_kernel(xl_ref, xr_ref, out_ref, lx, rx):
    blocks, _, rows, _ = out_ref.shape
    rank, span = LANES, rows // 2
    for b in range(blocks):
        yl, core = b // CORES, b % CORES
        taken = pl.ds(yl * span, span)
        for i in range(2):
            put = pl.ds(b * rows + i * span, span)
            for half in range(2):
                near = (2 * half + i) * CORES + core
                lanes = slice(half * rank, (half + 1) * rank)
                lx[put, lanes] = xl_ref[near, taken]
                rx[put, lanes] = xr_ref[near, taken]
    for r in range(0, blocks, 2):
        right = rx[r * rows : (r + 2) * rows]
        for b in range(0, blocks, 2):
            sims = lax.dot_general(
                lx[b * rows : (b + 2) * rows], right, (((1,), (1,)), ((), ())), preferred_element_type=F32
            )
            for i in range(2):
                for j in range(2):
                    out_ref[b + i, r + j] = sims[i * rows : (i + 1) * rows, j * rows : (j + 1) * rows]


def sim_call(rows, left_x, right_x):
    operand = pltpu.VMEM((PARTS * rows, 2 * LANES), BF)
    return pl.pallas_call(
        sim_kernel,
        out_shape=jax.ShapeDtypeStruct((PARTS, PARTS, rows, rows), F32),
        in_specs=[VMEM, VMEM],
        out_specs=VMEM,
        scratch_shapes=[operand, operand],
        compiler_params=pltpu.CompilerParams(vmem_limit_bytes=24 << 20),
        cost_estimate=pl.CostEstimate(
            flops=4 * PARTS * PARTS * rows * rows * LANES, bytes_accessed=4 << 20, transcendentals=0
        ),
    )(left_x, right_x)


def sub_epoch_kernel(step_size, level, last, table_ref, mask_ref, sim_ref, *refs):
    if level == 0:
        all_ref, *refs = refs
    else:
        left_ref, right_ref, *refs = refs
    *outs, ls, lb, rs0, rb0, rs1, rb1, mf, kr, ks = refs
    blocks, rows, rank = ls.shape
    part, node = table_ref[INFO], table_ref[INFO + SUB + level]
    flip = jnp.int32(0) if level == 0 else table_ref[INFO + level]

    def place(slot):
        return slot if level == 0 else jnp.where(flip == 1, blocks - 1 - slot, slot)

    mf[...] = mask_ref[...].astype(F32)
    for b in range(blocks):
        row, lane = mask_place(node, b)
        kr[pl.ds(b, 1)] = mf[node // ZS % XS * CORES + b % CORES, pl.ds(row, 1)]
    values = kr[...]
    lanes = lax.broadcasted_iota(jnp.int32, values.shape, 1)
    for c in range(blocks):
        mine = jnp.where(lanes == lane + level * PARTS + c, values, 0.0)
        ks[c] = jnp.broadcast_to(step_size * jnp.sum(mine, axis=1, keepdims=True), values.shape)

    span = rows // 2
    for b in range(blocks):
        if level == 0:
            yl, core = b // CORES, b % CORES
            moved = pl.ds((YL + yl) * span, span)
            left = jnp.concatenate([all_ref[core, moved], all_ref[CORES + core, moved]]).astype(F32)
            right = jnp.concatenate([all_ref[2 * CORES + core, moved], all_ref[3 * CORES + core, moved]])
        else:
            left, right = left_ref[place(b)], right_ref[place(b)]
        right = right.astype(F32).T
        ls[b], rs0[b] = left, right
        lb[b], rb0[b] = left.astype(BF), right.astype(BF)

    def cycle_step(step, source, target, spots):
        (rs, rb), (rs_next, rb_next) = source, target
        preds = [jnp.dot(lb[b], rb[b], preferred_element_type=F32) for b in spots]
        resids = []
        for b, pred in zip(spots, preds):
            left, right = place(b), place(lax.rem(b + blocks - step, blocks))
            row = jnp.where(flip == 1, right, left)
            col = jnp.where(flip == 1, left, right)
            resids.append((ks[col, pl.ds(row, 1)] * (pred - sim_ref[left, right])).astype(BF))
        grads_l = [
            lax.dot_general(resid, rb[b], (((1,), (1,)), ((), ())), preferred_element_type=F32)
            for b, resid in zip(spots, resids)
        ]
        grads_r = [
            lax.dot_general(lb[b], resid, (((0,), (0,)), ((), ())), preferred_element_type=F32)
            for b, resid in zip(spots, resids)
        ]
        for b, grad in zip(spots, grads_l):
            new_left = ls[b] - grad
            ls[b] = new_left
            lb[b] = new_left.astype(BF)
        for b, grad in zip(spots, grads_r):
            new_right = rs[b] - grad
            after = (b + 1) % blocks if isinstance(b, int) else lax.rem(b + 1, blocks)
            rs_next[after] = new_right
            rb_next[after] = new_right.astype(BF)

    turns = ((rs0, rb0), (rs1, rb1))
    every = list(range(blocks))
    if last:
        for step in range(blocks):
            count = blocks + 1 - step
            mine = [lax.rem(place(part) + blocks - i, blocks) for i in range(count)]
            cycle_step(step, turns[step % 2], turns[1 - step % 2], every if count >= blocks else mine)
    else:

        def two_steps(pair, carry):
            cycle_step(2 * pair, *turns, every)
            cycle_step(2 * pair + 1, *turns[::-1], every)
            return carry

        lax.fori_loop(0, blocks // 2, two_steps, 0)
    if last:
        uo_ref, vo_ref = outs

        @pl.when(flip == 0)
        def _():
            uo_ref[...] = ls[place(part)]
            vo_ref[...] = rs0[place(part)].T

        @pl.when(flip == 1)
        def _():
            uo_ref[...] = rs0[place(part)].T
            vo_ref[...] = ls[place(part)]
    else:
        kept_ref, sent_ref = outs
        same = table_ref[INFO + 1 + level] == flip

        @pl.when(same)
        def _():
            for b in range(blocks):
                kept_ref[place(b)] = ls[b]
                sent_ref[place(b)] = lb[b]

        @pl.when(jnp.logical_not(same))
        def _():
            for b in range(blocks):
                right = rs0[b].T
                kept_ref[place(b)] = right
                sent_ref[place(b)] = right.astype(BF)


def sub_epoch_call(level, rows, table, mask, sims, *arrays):
    rank, last = LANES, level + 1 == SUB
    whole = (PARTS, rows, rank)
    if last:
        outs = (jax.ShapeDtypeStruct((rows, rank), F32),) * 2
    else:
        outs = (jax.ShapeDtypeStruct(whole, F32), jax.ShapeDtypeStruct(whole, BF))
    return pl.pallas_call(
        functools.partial(sub_epoch_kernel, 4.0 / rows, level, last),
        out_shape=outs,
        in_specs=[SMEM] + [VMEM] * (2 + len(arrays)),
        out_specs=(VMEM, VMEM),
        scratch_shapes=[pltpu.VMEM(whole, F32), pltpu.VMEM(whole, BF)] * 3
        + [
            pltpu.VMEM(mask.shape, F32),
            pltpu.VMEM((PARTS, LANES), F32),
            pltpu.VMEM((PARTS, PARTS, LANES), F32),
        ],
        compiler_params=pltpu.CompilerParams(vmem_limit_bytes=28 << 20),
        cost_estimate=pl.CostEstimate(
            flops=2 * PARTS * PARTS * rows * rows * 3 * rank,
            bytes_accessed=6 << 20,
            transcendentals=0,
        ),
    )(table, mask, sims, *arrays)


def swapped(array, stride):
    return lax.ppermute(array, BLK, [(i, i ^ stride) for i in range(PARTS)])


def spread(array, axes):
    return lax.all_to_all(array, axes, split_axis=0, concat_axis=0, tiled=True)


def local(features, factor_u, factor_v, tile_mask, matching):
    group = lax.axis_index(GRP).astype(jnp.int32)
    part = lax.axis_index(BLK).astype(jnp.int32)
    slot_rows, rank = factor_u.shape
    bits = [part // stride % 2 for stride in STRIDES]

    pieces = spread(pack_call(features, factor_u, factor_v).reshape(GROUPS, PIECE, rank), GRP)
    table = tables_call(jnp.stack([group, part]), matching, tile_mask)
    got = spread(pick_call(table, pieces), FAR)
    got = spread(regroup_call(got), NEAR).reshape(XS * CORES, -1, rank)
    half = YL * slot_rows // 2
    x0, mask = got[:, :half], got[:, 2 * half :]

    def work(level, sims, *arrays):
        return sub_epoch_call(level, slot_rows, table, mask, sims, *arrays)

    away, next_bit = STRIDES[1], [b // STRIDES[1] % 2 for b in range(PARTS)]
    first = lax.ppermute(x0, BLK, [(b, b ^ away) for b in range(PARTS) if b % CORES == next_bit[b]])
    y0 = swapped(x0, STRIDES[0])
    sims = sim_call(slot_rows, got, got)
    x1 = jnp.where(bits[1] == bits[0], x0, y0)
    kept, sent = work(0, sims, got)
    right = swapped(sent, STRIDES[0])
    sims = sim_call(slot_rows, x0, y0)
    right, first = lax.optimization_barrier((right, first))
    second = lax.ppermute(first, BLK, [(b, b ^ STRIDES[0]) for b in range(PARTS) if b % CORES != next_bit[b]])
    kept, sent = work(1, sims, kept, right)
    right = swapped(sent, STRIDES[1])
    y1 = jnp.where(bits[0] == bits[1], second, first)
    sims = sim_call(slot_rows, x1, y1)
    x2 = jnp.where(bits[2] == bits[1], x1, y1)
    y2 = swapped(x2, STRIDES[2])
    kept, sent = work(2, sims, kept, right)
    right = swapped(sent, STRIDES[2])
    kept, y2 = lax.optimization_barrier((kept, y2))
    return work(3, sim_call(slot_rows, x2, y2), kept, right)


def solution(mesh):
    fine = Mesh(mesh.devices.reshape(YH, XS, ZS, YL, CORES), ALL)
    in_specs = (P(ALL, None), P(ALL, None), P(ALL, None), P(ALL, None), P())
    out_specs = (P(ALL, None), P(ALL, None))
    return jax.shard_map(local, mesh=fine, in_specs=in_specs, out_specs=out_specs, check_vma=False)
```

```python
import functools

import jax
import jax.numpy as jnp
from jax import lax
from jax.experimental import pallas as pl
from jax.experimental.pallas import tpu as pltpu
from jax.sharding import Mesh, PartitionSpec as P

SUB = 4
GRP = ("yh", "x", "z")
BLK = ("yl", "core")
ALL = GRP + BLK
FAR = ("yh", "yl", "z")
NEAR = ("x", "core")
YH, XS, ZS, YL, CORES = 2, 4, 8, 4, 2
GROUPS, PARTS = YH * XS * ZS, YL * CORES
BF = jnp.bfloat16
F32 = jnp.float32
LANES = 128
PIECE = 8
STRIDES = (1, 2 * CORES, CORES)
INFO = GROUPS * PARTS
VALUES = INFO + 16
SMEM = pl.BlockSpec(memory_space=pltpu.SMEM)
VMEM = pl.BlockSpec(memory_space=pltpu.VMEM)


def pack_kernel(x_ref, u_ref, v_ref, out_ref):
    rows, rank = u_ref.shape
    out_ref[:rows] = x_ref[:, :rank].astype(BF)
    out_ref[rows : 2 * rows] = x_ref[:, rank:].astype(BF)
    out_ref[2 * rows : 3 * rows] = u_ref[...].astype(BF)
    out_ref[3 * rows :] = v_ref[...].astype(BF)


def pack_call(features, factor_u, factor_v):
    rows, rank = factor_u.shape
    return pl.pallas_call(
        pack_kernel,
        out_shape=jax.ShapeDtypeStruct((4 * rows, rank), BF),
        in_specs=[VMEM] * 3,
        out_specs=VMEM,
        cost_estimate=pl.CostEstimate(flops=100000, bytes_accessed=400000, transcendentals=0),
    )(features, factor_u, factor_v)


def mask_place(group, part):
    z = group % ZS
    return (group // (XS * ZS) * YL + part // CORES) * 2 + z // 4, (z % 4) * SUB * PARTS


def tables_kernel(here_ref, matching_ref, mask_ref, table_ref, inv_ref):
    group, part = here_ref[0], here_ref[1]

    def invert(e, carry):
        for t in range(SUB - 1):
            inv_ref[t * GROUPS + matching_ref[t, e]] = e
        return carry

    lax.fori_loop(0, GROUPS, invert, 0, unroll=4)

    def before(t, e):
        return inv_ref[t * GROUPS + e]

    def trace_back(d, carry):
        nodes = [d]
        for t in range(SUB - 2, -1, -1):
            nodes = [n for e in nodes for n in (e, before(t, e))]
        base = (d // (XS * ZS) * YL * ZS + d % ZS) * PARTS + d // ZS % XS * CORES
        for k in range(PARTS):
            yl, core = k // 2 % 2 * 2 + k // 4, k % 2
            table_ref[base + yl * ZS * PARTS + core] = nodes[k]
        return carry

    lax.fori_loop(0, GROUPS, trace_back, 0, unroll=2)

    table_ref[INFO] = part
    node = group
    for t in range(SUB - 1, -1, -1):
        table_ref[INFO + SUB + t] = node
        if t > 0:
            bit = part // STRIDES[t - 1] % 2
            table_ref[INFO + t] = bit
            node = jnp.where(bit == 1, before(t - 1, node), node)
    table_ref[INFO + 2 * SUB] = group
    for t in range(SUB):
        held = group
        for s in range(t - 1, -1, -1):
            held = before(s, held)
        for c in range(PARTS):
            table_ref[VALUES + t * PARTS + c] = mask_ref[0, held * PARTS + c]


def tables_call(here, matching, mask):
    return pl.pallas_call(
        tables_kernel,
        out_shape=jax.ShapeDtypeStruct((VALUES + SUB * PARTS,), jnp.int32),
        in_specs=[SMEM, SMEM, SMEM],
        out_specs=SMEM,
        scratch_shapes=[pltpu.SMEM((GROUPS * (SUB - 1),), jnp.int32)],
        cost_estimate=pl.CostEstimate(flops=2000000, bytes_accessed=4096, transcendentals=0),
    )(here, matching, mask)


def pick_kernel(table_ref, pieces_ref, out_ref):
    row, lane = mask_place(table_ref[INFO + 2 * SUB], table_ref[INFO])
    lanes = lax.broadcasted_iota(jnp.int32, (PIECE, LANES), 1)
    values = jnp.zeros((PIECE, LANES), jnp.int32)
    for i in range(SUB * PARTS):
        values = jnp.where(lanes == lane + i, table_ref[VALUES + i], values)
    rows = lax.broadcasted_iota(jnp.int32, (PIECE, LANES), 0)
    tile = jnp.where(rows == row % PIECE, values, 0).astype(F32).astype(BF)

    def one(far, carry):
        for near in range(XS * CORES):
            out_ref[far, near] = pieces_ref[table_ref[far * XS * CORES + near]]
        out_ref[far, XS * CORES] = tile
        return carry

    lax.fori_loop(0, out_ref.shape[0], one, 0, unroll=4)


def pick_call(table, pieces):
    return pl.pallas_call(
        pick_kernel,
        out_shape=jax.ShapeDtypeStruct((YH * YL * ZS, XS * CORES + 1, PIECE, LANES), BF),
        in_specs=[SMEM, VMEM],
        out_specs=VMEM,
        compiler_params=pltpu.CompilerParams(vmem_limit_bytes=16 << 20),
        cost_estimate=pl.CostEstimate(flops=1000000, bytes_accessed=2 << 20, transcendentals=0),
    )(table, pieces)


def regroup_kernel(got_ref, out_ref):
    far = YH * YL * ZS
    for near in range(XS * CORES):
        out_ref[near, :far] = got_ref[:, near]
    for yh in range(YH):
        span = far // YH
        total = jnp.sum(got_ref[yh * span : (yh + 1) * span, XS * CORES].astype(F32), axis=0).astype(BF)
        for near in range(XS * CORES):
            out_ref[near, far + yh] = total


def regroup_call(got):
    return pl.pallas_call(
        regroup_kernel,
        out_shape=jax.ShapeDtypeStruct((XS * CORES, YH * YL * ZS + YH, PIECE, LANES), BF),
        in_specs=[VMEM],
        out_specs=VMEM,
        compiler_params=pltpu.CompilerParams(vmem_limit_bytes=16 << 20),
        cost_estimate=pl.CostEstimate(flops=1000000, bytes_accessed=2 << 20, transcendentals=0),
    )(got)


def sim_kernel(level, table_ref, mask_ref, xl_ref, xr_ref, out_ref, ks, lx, rx, mf, kr):
    blocks, _, rows, _ = out_ref.shape
    rank, span, step_size = LANES, rows // 2, 4.0 / rows
    node = table_ref[INFO + SUB + level]
    mf[...] = mask_ref[...].astype(F32)
    for b in range(blocks):
        row, lane = mask_place(node, b)
        kr[pl.ds(b, 1)] = mf[node // ZS % XS * CORES + b % CORES, pl.ds(row, 1)]
    values = kr[...]
    lanes = lax.broadcasted_iota(jnp.int32, values.shape, 1)
    for c in range(blocks):
        mine = jnp.where(lanes == lane + level * PARTS + c, values, 0.0)
        ks[c] = jnp.broadcast_to(step_size * jnp.sum(mine, axis=1, keepdims=True), values.shape)

    for b in range(blocks):
        yl, core = b // CORES, b % CORES
        taken = pl.ds(yl * span, span)
        for i in range(2):
            put = pl.ds(b * rows + i * span, span)
            for half in range(2):
                near = (2 * half + i) * CORES + core
                lanes = slice(half * rank, (half + 1) * rank)
                lx[put, lanes] = xl_ref[near, taken]
                rx[put, lanes] = xr_ref[near, taken]
    for r in range(0, blocks, 2):
        right = rx[r * rows : (r + 2) * rows]
        for b in range(0, blocks, 2):
            sims = lax.dot_general(
                lx[b * rows : (b + 2) * rows], right, (((1,), (1,)), ((), ())), preferred_element_type=F32
            )
            for i in range(2):
                for j in range(2):
                    out_ref[b + i, r + j] = sims[i * rows : (i + 1) * rows, j * rows : (j + 1) * rows]


def sim_call(level, rows, table, mask, left_x, right_x):
    operand = pltpu.VMEM((PARTS * rows, 2 * LANES), BF)
    return pl.pallas_call(
        functools.partial(sim_kernel, level),
        out_shape=(
            jax.ShapeDtypeStruct((PARTS, PARTS, rows, rows), F32),
            jax.ShapeDtypeStruct((PARTS, PARTS, LANES), F32),
        ),
        in_specs=[SMEM, VMEM, VMEM, VMEM],
        out_specs=(VMEM, VMEM),
        scratch_shapes=[operand, operand, pltpu.VMEM(mask.shape, F32), pltpu.VMEM((PARTS, LANES), F32)],
        compiler_params=pltpu.CompilerParams(vmem_limit_bytes=24 << 20),
        cost_estimate=pl.CostEstimate(
            flops=4 * PARTS * PARTS * rows * rows * LANES, bytes_accessed=4 << 20, transcendentals=0
        ),
    )(table, mask, left_x, right_x)


def sub_epoch_kernel(level, last, table_ref, ks, sim_ref, *refs):
    if level == 0:
        all_ref, *refs = refs
    else:
        left_ref, right_ref, *refs = refs
    *outs, ls, lb, rs0, rb0, rs1, rb1 = refs
    blocks, rows, rank = ls.shape
    part = table_ref[INFO]
    flip = jnp.int32(0) if level == 0 else table_ref[INFO + level]

    def place(slot):
        return slot if level == 0 else jnp.where(flip == 1, blocks - 1 - slot, slot)

    span = rows // 2
    for b in range(blocks):
        if level == 0:
            yl, core = b // CORES, b % CORES
            moved = pl.ds((YL + yl) * span, span)
            left = jnp.concatenate([all_ref[core, moved], all_ref[CORES + core, moved]]).astype(F32)
            right = jnp.concatenate([all_ref[2 * CORES + core, moved], all_ref[3 * CORES + core, moved]])
        else:
            left, right = left_ref[place(b)], right_ref[place(b)]
        right = right.astype(F32).T
        ls[b], rs0[b] = left, right
        lb[b], rb0[b] = left.astype(BF), right.astype(BF)

    def cycle_step(step, source, target, spots):
        (rs, rb), (rs_next, rb_next) = source, target
        preds = [jnp.dot(lb[b], rb[b], preferred_element_type=F32) for b in spots]
        resids = []
        for b, pred in zip(spots, preds):
            left, right = place(b), place(lax.rem(b + blocks - step, blocks))
            row = jnp.where(flip == 1, right, left)
            col = jnp.where(flip == 1, left, right)
            resids.append((ks[col, pl.ds(row, 1)] * (pred - sim_ref[left, right])).astype(BF))
        grads_l = [
            lax.dot_general(resid, rb[b], (((1,), (1,)), ((), ())), preferred_element_type=F32)
            for b, resid in zip(spots, resids)
        ]
        grads_r = [
            lax.dot_general(lb[b], resid, (((0,), (0,)), ((), ())), preferred_element_type=F32)
            for b, resid in zip(spots, resids)
        ]
        for b, grad in zip(spots, grads_l):
            new_left = ls[b] - grad
            ls[b] = new_left
            lb[b] = new_left.astype(BF)
        for b, grad in zip(spots, grads_r):
            new_right = rs[b] - grad
            after = (b + 1) % blocks if isinstance(b, int) else lax.rem(b + 1, blocks)
            rs_next[after] = new_right
            rb_next[after] = new_right.astype(BF)

    turns = ((rs0, rb0), (rs1, rb1))
    every = list(range(blocks))
    if last:
        for step in range(blocks):
            count = blocks + 1 - step
            mine = [lax.rem(place(part) + blocks - i, blocks) for i in range(count)]
            cycle_step(step, turns[step % 2], turns[1 - step % 2], every if count >= blocks else mine)
    else:

        def two_steps(pair, carry):
            cycle_step(2 * pair, *turns, every)
            cycle_step(2 * pair + 1, *turns[::-1], every)
            return carry

        lax.fori_loop(0, blocks // 2, two_steps, 0)
    if last:
        uo_ref, vo_ref = outs

        @pl.when(flip == 0)
        def _():
            uo_ref[...] = ls[place(part)]
            vo_ref[...] = rs0[place(part)].T

        @pl.when(flip == 1)
        def _():
            uo_ref[...] = rs0[place(part)].T
            vo_ref[...] = ls[place(part)]
    else:
        kept_ref, sent_ref = outs
        same = table_ref[INFO + 1 + level] == flip

        @pl.when(same)
        def _():
            for b in range(blocks):
                kept_ref[place(b)] = ls[b]
                sent_ref[place(b)] = lb[b]

        @pl.when(jnp.logical_not(same))
        def _():
            for b in range(blocks):
                right = rs0[b].T
                kept_ref[place(b)] = right
                sent_ref[place(b)] = right.astype(BF)


def sub_epoch_call(level, rows, table, keeps, sims, *arrays):
    rank, last = LANES, level + 1 == SUB
    whole = (PARTS, rows, rank)
    if last:
        outs = (jax.ShapeDtypeStruct((rows, rank), F32),) * 2
    else:
        outs = (jax.ShapeDtypeStruct(whole, F32), jax.ShapeDtypeStruct(whole, BF))
    return pl.pallas_call(
        functools.partial(sub_epoch_kernel, level, last),
        out_shape=outs,
        in_specs=[SMEM] + [VMEM] * (2 + len(arrays)),
        out_specs=(VMEM, VMEM),
        scratch_shapes=[pltpu.VMEM(whole, F32), pltpu.VMEM(whole, BF)] * 3,
        compiler_params=pltpu.CompilerParams(vmem_limit_bytes=28 << 20),
        cost_estimate=pl.CostEstimate(
            flops=2 * PARTS * PARTS * rows * rows * 3 * rank,
            bytes_accessed=6 << 20,
            transcendentals=0,
        ),
    )(table, keeps, sims, *arrays)


def swapped(array, stride):
    return lax.ppermute(array, BLK, [(i, i ^ stride) for i in range(PARTS)])


def spread(array, axes):
    return lax.all_to_all(array, axes, split_axis=0, concat_axis=0, tiled=True)


def local(features, factor_u, factor_v, tile_mask, matching):
    group = lax.axis_index(GRP).astype(jnp.int32)
    part = lax.axis_index(BLK).astype(jnp.int32)
    slot_rows, rank = factor_u.shape
    bits = [part // stride % 2 for stride in STRIDES]

    pieces = spread(pack_call(features, factor_u, factor_v).reshape(GROUPS, PIECE, rank), GRP)
    table = tables_call(jnp.stack([group, part]), matching, tile_mask)
    got = spread(pick_call(table, pieces), FAR)
    got = spread(regroup_call(got), NEAR).reshape(XS * CORES, -1, rank)
    half = YL * slot_rows // 2
    x0, mask = got[:, :half], got[:, 2 * half :]

    def work(level, sims, *arrays):
        return sub_epoch_call(level, slot_rows, table, sims[1], sims[0], *arrays)

    away, next_bit = STRIDES[1], [b // STRIDES[1] % 2 for b in range(PARTS)]
    first = lax.ppermute(x0, BLK, [(b, b ^ away) for b in range(PARTS) if b % CORES == next_bit[b]])
    y0 = swapped(x0, STRIDES[0])
    sims = sim_call(0, slot_rows, table, mask, got, got)
    x1 = jnp.where(bits[1] == bits[0], x0, y0)
    kept, sent = work(0, sims, got)
    right = swapped(sent, STRIDES[0])
    sims = sim_call(1, slot_rows, table, mask, x0, y0)
    right, first = lax.optimization_barrier((right, first))
    second = lax.ppermute(first, BLK, [(b, b ^ STRIDES[0]) for b in range(PARTS) if b % CORES != next_bit[b]])
    kept, sent = work(1, sims, kept, right)
    right = swapped(sent, STRIDES[1])
    y1 = jnp.where(bits[0] == bits[1], second, first)
    sims = sim_call(2, slot_rows, table, mask, x1, y1)
    x2 = jnp.where(bits[2] == bits[1], x1, y1)
    y2 = swapped(x2, STRIDES[2])
    kept, sent = work(2, sims, kept, right)
    right = swapped(sent, STRIDES[2])
    kept, y2 = lax.optimization_barrier((kept, y2))
    return work(3, sim_call(3, slot_rows, table, mask, x2, y2), kept, right)


def solution(mesh):
    fine = Mesh(mesh.devices.reshape(YH, XS, ZS, YL, CORES), ALL)
    in_specs = (P(ALL, None), P(ALL, None), P(ALL, None), P(ALL, None), P())
    out_specs = (P(ALL, None), P(ALL, None))
    return jax.shard_map(local, mesh=fine, in_specs=in_specs, out_specs=out_specs, check_vma=False)
```
